32 devices in a mesh: band: 8 (over z, y), batch: 4 (over x, core).
Axes of the slice: x: 2, y: 2, z: 4, core: 2. Of those that a mesh axis runs over, the one named last changes fastest.
Arguments:
- tiles: bfloat16 [8, 128, 128, 128], P('band'), may hold values from -256 to 256, as said below
- tile_row: int32 [8, 128], P('band'), may hold values from 0 to 3, as said below
- tile_col: int32 [8, 128], P('band'), may hold values from 0 to 15, as said below
- tile_count: int32 [8], P('band'), may hold values from 80 to 128, as said below
- cost: float32 [8, 2048], P('batch', 'band'), may hold values from -6 to 6
- bound_vec: float32 [4096], P('band'), may hold values from -6 to 6
- x_start: float32 [8, 2048], P('batch', 'band'), may hold values from 0 to 1
- y_start: float32 [8, 4096], P('batch', 'band'), may hold values from 0 to 1
Outputs:
- x_out: float32 [8, 2048], P('batch', 'band')
- y_out: float32 [8, 4096], P('batch', 'band')
The draws below stay inside these ranges and needn't reach their ends.
Inputs may be any that keep to these rules, and one draw needn't show every extreme that they name: `tile_row`: within a band, tiles 0 to 3 lie in row blocks 0 to 3 in order. `tile_col`: the owner of column block k is band k // 2. Among a band's live tiles at most 32 have one owner, and the tiles of one owner stand in a row; tiles 0 to 1 of band b lie in column blocks b * 2 + t, so each band gives exactly 32 tiles to its own owner and every row block and column block holds a live tile. `tile_count`: one band in every draw is full. `tiles`: every entry has magnitude 0.1 or more.
All inputs are finite; a program needn't handle non-finite values.
Results may differ from the reference program's by a relative error of at most 0.0003.
Values sent between devices are 32-bit elements; how exact they have to be, the bound alone decides.
No kernel may reach another device: no remote copies, remote signals or barrier semaphores. Data moves between devices by JAX's collectives and lax.ppermute only.
A program may use at most 64 MiB of HBM per device.

```python
import math
import jax
import jax.numpy as jnp
from jax import lax

TILE = 128
TILES = 128
ROWBLK = 4
COLBLK = 2
COSTS = 8
BANDS = 8
CAPACITY = 32
NROW = 4096
NCOL = 2048


def pattern(key):
    base = jax.random.fold_in(key, 7)
    band_keys = jax.random.split(base, BANDS)

    def one_band(band_key, band):
        key_perm, key_counts, key_cols, key_rows = jax.random.split(band_key, 4)
        shuffled = jax.random.permutation(key_perm, BANDS).astype(jnp.int32)
        where_band = jnp.argmax(shuffled == band)
        owners = shuffled.at[where_band].set(shuffled[0]).at[0].set(band)
        lowest = max(1, CAPACITY // 2)
        group_sizes = jax.random.randint(key_counts, (BANDS,), lowest, CAPACITY + 1).astype(jnp.int32).at[0].set(CAPACITY)
        starts = jnp.cumsum(group_sizes) - group_sizes
        indices = jnp.arange(TILES, dtype=jnp.int32)
        group = (jnp.sum((starts[None, :] <= indices[:, None]).astype(jnp.int32), axis=1) - 1).astype(jnp.int32)
        owner_of = owners[group]
        tile_cols = owner_of * COLBLK + jax.random.randint(key_cols, (TILES,), 0, COLBLK).astype(jnp.int32)
        tile_cols = jnp.where(indices < COLBLK, band * COLBLK + indices, tile_cols)
        tile_rows = jax.random.randint(key_rows, (TILES,), 0, ROWBLK).astype(jnp.int32)
        tile_rows = jnp.where(indices < ROWBLK, indices, tile_rows)
        return (tile_rows, tile_cols)
    tile_rows, tile_cols = jax.vmap(one_band)(band_keys, jnp.arange(BANDS, dtype=jnp.int32))
    key_live, key_full = jax.random.split(jax.random.fold_in(base, 11))
    lowest_count = max(5 * TILES // 8, ROWBLK, COLBLK)
    live_count = jax.random.randint(key_live, (BANDS,), lowest_count, TILES + 1).astype(jnp.int32)
    full_band = jax.random.randint(key_full, (), 0, BANDS)
    live_count = live_count.at[full_band].set(TILES)
    return (tile_rows, tile_cols, live_count)


def draw_tile_row(key, part):
    return pattern(key)[0]


def draw_tile_col(key, part):
    return pattern(key)[1]


def draw_tile_count(key, part):
    return pattern(key)[2]


def draw_tiles(key, part):
    key_sign, key_mag, key_row, key_col = jax.random.split(key, 4)
    shape = (BANDS, TILES, TILE, TILE)
    signs = jnp.where(jax.random.uniform(key_sign, shape) < 0.5, -1.0, 1.0)
    magnitude = jnp.exp(jax.random.uniform(key_mag, shape, jnp.float32, math.log(0.1), 0.0))
    spread = math.log(10.0)
    row_factor = jnp.exp(jax.random.uniform(key_row, (BANDS, TILES, TILE, 1), jnp.float32, 0.0, spread))
    col_factor = jnp.exp(jax.random.uniform(key_col, (BANDS, TILES, 1, TILE), jnp.float32, 0.0, spread))
    return (signs * magnitude * row_factor * col_factor).astype(jnp.bfloat16)


def block_scale(key, dims, pieces, smallest, high):
    level, own = 1.0, jax.random.fold_in(key, 6)
    for position, blocks in pieces:
        draws = jnp.exp(jax.random.uniform(jax.random.fold_in(own, position), (blocks,), jnp.float32, smallest / len(pieces), high / len(pieces)))
        level = level * jnp.repeat(draws, dims[position] // blocks).reshape([-1 if axis == position else 1 for axis in range(len(dims))])
    return level


def noise(stream_key, dims, scale, reach, pieces=(), kind=jnp.bfloat16):
    entries = jax.random.normal(stream_key, dims, jnp.float32) * scale
    if len(pieces) > 0:
        entries = block_scale(stream_key, dims, pieces, -0.22, 0.18) * entries
    return jnp.clip(entries, min=-reach, max=reach).astype(kind)


def setup_inputs(seed: int = 0) -> dict:
    arg_keys = jax.random.split(jax.random.key(seed), 9)
    return {
        "tiles": draw_tiles(jax.random.fold_in(arg_keys[8], 71), 0),
        "tile_row": draw_tile_row(jax.random.fold_in(arg_keys[8], 71), 0),
        "tile_col": draw_tile_col(jax.random.fold_in(arg_keys[8], 71), 0),
        "tile_count": draw_tile_count(jax.random.fold_in(arg_keys[8], 71), 0),
        "cost": noise(arg_keys[4], (COSTS, NCOL), 1.0, 6.0, ((0, 4), (1, 8)), jnp.float32),
        "bound_vec": noise(arg_keys[5], (NROW,), 1.0, 6.0, ((0, 8),), jnp.float32),
        "x_start": jnp.clip(1.0 * jax.random.uniform(arg_keys[6], (COSTS, NCOL), jnp.float32) ** block_scale(arg_keys[6], (COSTS, NCOL), ((0, 4), (1, 8)), -0.2, 0.2), 0.0, 1.0),
        "y_start": jnp.clip(1.0 * jax.random.uniform(arg_keys[7], (COSTS, NROW), jnp.float32) ** block_scale(arg_keys[7], (COSTS, NROW), ((0, 4), (1, 8)), -0.2, 0.2), 0.0, 1.0),
    }


step_size = 0.0625
high = lax.Precision.HIGHEST

def reference(tiles, tile_row, tile_col, tile_count, cost, bound_vec, x_start, y_start):
    band_count = tiles.shape[0]
    tile_edge = tiles.shape[2]
    indices = jnp.arange(tiles.shape[1], dtype=jnp.int32)
    live = indices[None, :] < tile_count[:, None]
    rowsel = (tile_row[:, None, :] == jnp.arange(ROWBLK, dtype=jnp.int32)[None, :, None]) & live[:, None, :]

    def row_peaks(args):
        block, select, alive = args
        magnitude = jnp.abs(block.astype(jnp.float32))
        row_max = jnp.where(alive[:, None], lax.optimization_barrier(jnp.max(magnitude, axis=2)), 0.0)
        return lax.optimization_barrier(jnp.max(jnp.where(select[:, :, None], row_max[None], 0.0), axis=1))
    rscale = lax.rsqrt(lax.map(row_peaks, (tiles, rowsel, live)))

    def col_peaks(args):
        block, tile_rows, alive, scales = args
        spread = scales[tile_rows]
        peak = lax.optimization_barrier(jnp.max(jnp.abs(block.astype(jnp.float32)) * spread[:, :, None], axis=1))
        return jnp.where(alive[:, None], peak, 0.0)
    col_tile = lax.map(col_peaks, (tiles, tile_row, live, rscale))
    col_max = jnp.zeros((COLBLK * band_count, tile_edge), jnp.float32).at[tile_col.reshape(-1)].max(col_tile.reshape(-1, tile_edge))
    cscale = lax.rsqrt(col_max).reshape(-1)
    rflat = rscale.reshape(-1)

    def forward(vec):
        scaled = (vec * cscale).reshape(vec.shape[0], COLBLK * band_count, tile_edge)

        def one_band(args):
            block, tile_cols, alive, select = args
            picked = jnp.take(scaled, tile_cols, axis=1)
            product = jnp.einsum('tij,ktj->tki', block.astype(jnp.float32), picked, precision=high)
            product = jnp.where(alive[:, None, None], product, 0.0)
            return jnp.einsum('rt,tki->kri', select.astype(jnp.float32), product, precision=high)
        result = lax.map(one_band, (tiles, tile_col, live, rowsel))
        return jnp.transpose(result, (1, 0, 2, 3)).reshape(vec.shape[0], -1) * rflat

    def adjoint(vec):
        weighted = (vec * rflat).reshape(vec.shape[0], band_count, ROWBLK, tile_edge)

        def one_band(total, args):
            block, band_w, tile_cols, alive, select = args
            spread = jnp.einsum('rt,kri->tki', select.astype(jnp.float32), band_w, precision=high)
            partial_value = jnp.einsum('tij,tki->ktj', block.astype(jnp.float32), spread, precision=high)
            partial_value = jnp.where(alive[None, :, None], partial_value, 0.0)
            return (total.at[:, tile_cols].add(partial_value), None)
        start = jnp.zeros((vec.shape[0], COLBLK * band_count, tile_edge), jnp.float32)
        total, _unused = lax.scan(one_band, start, (tiles, jnp.moveaxis(weighted, 1, 0), tile_col, live, rowsel))
        return total.reshape(vec.shape[0], -1) * cscale
    scost = cost * cscale
    sbound = bound_vec * rflat
    primal_one = jnp.maximum(0.0, x_start - step_size * (scost - adjoint(y_start)))
    dual_one = jnp.maximum(0.0, y_start + step_size * (sbound - forward(2.0 * primal_one - x_start)))
    primal_step = lax.optimization_barrier(jnp.sum((primal_one - x_start) ** 2, axis=1, keepdims=True))
    dual_step = lax.optimization_barrier(jnp.sum((dual_one - y_start) ** 2, axis=1, keepdims=True))
    weight_ratio = jnp.sqrt((dual_step + 1e-06) / (primal_step + 1e-06))
    primal_two = jnp.maximum(0.0, primal_one - step_size / weight_ratio * (scost - adjoint(dual_one)))
    dual_two = jnp.maximum(0.0, dual_one + step_size * weight_ratio * (sbound - forward(2.0 * primal_two - primal_one)))
    return (primal_two, dual_two)
```

```python
import functools

import jax
import jax.numpy as jnp
from jax import lax
from jax.experimental import pallas as pl
from jax.experimental.pallas import tpu as pltpu
from jax.sharding import PartitionSpec as P

ROWBLK = 4
COLBLK = 2
EDGE = 128
VECS = 2
LEFT = 16
GROUP = 32
KEPT = 8

step_size = 0.0625


def split(value):
    high = value.astype(jnp.bfloat16).astype(jnp.float32)
    rest = value - high
    mid = rest.astype(jnp.bfloat16).astype(jnp.float32)
    low = (rest - mid).astype(jnp.bfloat16).astype(jnp.float32)
    return high, mid, low


def joined(rows):
    return rows[0:2] + rows[2:4] + rows[4:6]


def fetch(tiles_ref, held_ref, sems, g):
    group = pl.ds(g * GROUP, GROUP)
    return pltpu.make_async_copy(tiles_ref.at[group], held_ref.at[group], sems.at[g])


def row_of(rows_ref, count, t):
    return jnp.where(t < count, rows_ref[t], ROWBLK)


def products(multiply, place, stage_ref, into_ref, ntile):
    stage_ref[1] = jnp.zeros(stage_ref.shape[1:], jnp.float32)

    def group(g, carry):
        now = g % 2
        for u in range(GROUP):
            stage_ref[now, u] = multiply(g * GROUP + u)[0:KEPT]
        for u in range(GROUP):
            into_ref[place(jnp.maximum((g - 1) * GROUP + u, 0))] += stage_ref[1 - now, u]
        return carry

    groups = ntile // GROUP
    lax.fori_loop(0, groups, group, 0)
    for u in range(GROUP):
        into_ref[place(ntile - GROUP + u)] += stage_ref[(groups - 1) % 2, u]


def put_left(left32_ref, left_ref, index, value):
    for s, term in enumerate(split(value)):
        left32_ref[index, 2 * s : 2 * s + 2, :] = term
    left_ref[index] = left32_ref[index].astype(jnp.bfloat16)


def adjoint_start(sums_ref, cost_ref, band):
    sums_ref[...] = jnp.zeros_like(sums_ref)
    for j in range(COLBLK):
        sums_ref[band * COLBLK + j, 0:VECS, :] = -cost_ref[:, j * EDGE : (j + 1) * EDGE]


def adjoint_sum(sums_ref, v):
    blocks = sums_ref.shape[0]
    flat = sums_ref.reshape(blocks * KEPT, EDGE)
    return sum(flat[pl.ds(VECS * s + v, blocks, stride=KEPT), :] for s in range(3))


def forward_left(left32_ref, left_ref, v, value):
    blocks = left32_ref.shape[0]
    flat = left32_ref.reshape(blocks * LEFT, EDGE)
    for s, term in enumerate(split(value)):
        flat[pl.ds(VECS * s + v, blocks, stride=LEFT), :] = term


def forward_pass(rows_ref, cols_ref, live, held_ref, right_ref, stage_ref, out_ref):
    def multiply(t):
        return lax.dot_general(
            right_ref[cols_ref[t]],
            held_ref[t],
            (((1,), (1,)), ((), ())),
            preferred_element_type=jnp.float32,
        )

    out_ref[...] = jnp.zeros_like(out_ref)
    place = lambda t: row_of(rows_ref, live, t)
    products(multiply, place, stage_ref, out_ref, held_ref.shape[0])


def adjoint_pass(rows_ref, cols_ref, live, held_ref, left_ref, stage_ref, sums_ref):
    def multiply(t):
        r = row_of(rows_ref, live, t)
        return jnp.dot(left_ref[r], held_ref[t], preferred_element_type=jnp.float32)

    products(multiply, lambda t: cols_ref[t], stage_ref, sums_ref, held_ref.shape[0])


def scale_kernel(
    place_ref, rows_ref, cols_ref, count_ref, tiles_ref, y_ref, x_ref, cost_ref,
    send_ref, rscale_ref, held_ref,
    sems, peak_ref, spread_ref, left32_ref, left_ref, top_ref, stage_ref, sums_ref,
):
    ntile = held_ref.shape[0]
    blocks = top_ref.shape[0]
    live = count_ref[0]
    band = place_ref[0]
    groups = ntile // GROUP
    for g in range(groups):
        fetch(tiles_ref, held_ref, sems, g).start()
    peak_ref[...] = jnp.zeros_like(peak_ref)
    top_ref[...] = jnp.zeros_like(top_ref)
    left32_ref[...] = jnp.zeros_like(left32_ref)
    left_ref[ROWBLK] = jnp.zeros((LEFT, EDGE), jnp.bfloat16)
    spread_ref[ROWBLK] = jnp.zeros((EDGE, EDGE), jnp.float32)
    adjoint_start(sums_ref, cost_ref, band)

    def row_peaks(g, carry):
        fetch(tiles_ref, held_ref, sems, g).wait()
        for u in range(GROUP):
            t = g * GROUP + u
            r = row_of(rows_ref, live, t)
            peak_ref[r] = jnp.maximum(peak_ref[r], jnp.abs(held_ref[t]))
        return carry

    lax.fori_loop(0, groups, row_peaks, 0)

    for r in range(ROWBLK):
        peak = jnp.max(peak_ref[r].astype(jnp.float32), axis=1, keepdims=True)
        spread = jnp.broadcast_to(lax.rsqrt(peak), (EDGE, EDGE))
        spread_ref[r] = spread
        scale = spread.T[0:1, :]
        rscale_ref[r : r + 1, :] = scale
        put_left(left32_ref, left_ref, r, y_ref[:, r * EDGE : (r + 1) * EDGE] * scale)

    def multiply(t):
        r = row_of(rows_ref, live, t)
        c = cols_ref[t]
        tile = held_ref[t]
        scaled = jnp.abs(tile).astype(jnp.float32) * spread_ref[r]
        top_ref[c] = jnp.maximum(top_ref[c], jnp.max(scaled.reshape(EDGE // 8, 8, EDGE), axis=0))
        return jnp.dot(left_ref[r], tile, preferred_element_type=jnp.float32)

    products(multiply, lambda t: cols_ref[t], stage_ref, sums_ref, ntile)

    send_ref[0:blocks, :] = jnp.max(top_ref[...], axis=1)
    row = lax.broadcasted_iota(jnp.int32, (blocks, EDGE), 0)
    for v in range(VECS):
        send_ref[(1 + v) * blocks : (2 + v) * blocks, :] = adjoint_sum(sums_ref, v)
        own = jnp.zeros((blocks, EDGE), jnp.float32)
        for j in range(COLBLK):
            part = x_ref[v : v + 1, j * EDGE : (j + 1) * EDGE]
            own = jnp.where(row == band * COLBLK + j, part, own)
        send_ref[(3 + v) * blocks : (4 + v) * blocks, :] = own


def step_kernel(
    place_ref, rows_ref, cols_ref, count_ref, held_ref, got_ref, rscale_ref, y_ref, bound_ref, cost_ref,
    send_ref, x_one_ref, cscale_ref, y_one_ref, moved_ref,
    right32_ref, right_ref, out_ref, left32_ref, left_ref, stage_ref, sums_ref,
):
    blocks = right_ref.shape[0]
    live = count_ref[0]
    band = place_ref[0]
    right32_ref[...] = jnp.zeros_like(right32_ref)
    left32_ref[...] = jnp.zeros_like(left32_ref)
    left_ref[ROWBLK] = jnp.zeros((LEFT, EDGE), jnp.bfloat16)
    adjoint_start(sums_ref, cost_ref, band)

    cscale = lax.rsqrt(got_ref[0:blocks, :])
    cscale_ref[...] = cscale
    for v in range(VECS):
        total = got_ref[(1 + v) * blocks : (2 + v) * blocks, :]
        before = got_ref[(3 + v) * blocks : (4 + v) * blocks, :]
        after = jnp.maximum(0.0, before + step_size * (cscale * total))
        x_one_ref[v * blocks : (v + 1) * blocks, :] = after
        moved = jnp.sum(jnp.sum((after - before) ** 2, axis=0, keepdims=True), axis=1, keepdims=True)
        moved_ref[v : v + 1, :] = jnp.broadcast_to(moved, (1, EDGE))
        forward_left(right32_ref, right_ref, v, cscale * (2.0 * after - before))
    right_ref[...] = right32_ref[...].astype(jnp.bfloat16)

    forward_pass(rows_ref, cols_ref, live, held_ref, right_ref, stage_ref, out_ref)

    moved = jnp.zeros((VECS, EDGE), jnp.float32)
    for r in range(ROWBLK):
        span = slice(r * EDGE, (r + 1) * EDGE)
        scale = rscale_ref[r : r + 1, :]
        before = y_ref[:, span]
        after = jnp.maximum(
            0.0, before + step_size * (scale * (bound_ref[:, span] - joined(out_ref[r])))
        )
        y_one_ref[:, span] = after
        moved += (after - before) ** 2
        put_left(left32_ref, left_ref, r, after * scale)

    adjoint_pass(rows_ref, cols_ref, live, held_ref, left_ref, stage_ref, sums_ref)
    for v in range(VECS):
        send_ref[v * blocks : (v + 1) * blocks, :] = adjoint_sum(sums_ref, v)
    send_ref[VECS * blocks :, :] = jnp.zeros((8, EDGE), jnp.float32)
    send_ref[VECS * blocks : VECS * blocks + VECS, :] = moved


def last_kernel(
    place_ref, rows_ref, cols_ref, count_ref, held_ref, got_ref, rscale_ref, y_ref, bound_ref, x_one_ref, cscale_ref, moved_ref,
    x_out_ref, y_out_ref,
    right32_ref, right_ref, stage_ref, out_ref,
):
    blocks = right_ref.shape[0]
    live = count_ref[0]
    band = place_ref[0]
    right32_ref[...] = jnp.zeros_like(right32_ref)
    cscale = cscale_ref[...]
    row = lax.broadcasted_iota(jnp.int32, (blocks, EDGE), 0)
    dual = jnp.sum(got_ref[VECS * blocks : VECS * blocks + VECS, :], axis=1, keepdims=True)
    ratio = jnp.sqrt((dual + 1e-06) / (moved_ref[...] + 1e-06))
    for v in range(VECS):
        total = got_ref[v * blocks : (v + 1) * blocks, :]
        before = x_one_ref[v * blocks : (v + 1) * blocks, :]
        after = jnp.maximum(0.0, before + step_size / ratio[v : v + 1, :] * (cscale * total))
        for j in range(COLBLK):
            own = jnp.where(row == band * COLBLK + j, after, 0.0)
            x_out_ref[v : v + 1, j * EDGE : (j + 1) * EDGE] = jnp.sum(own, axis=0, keepdims=True)
        forward_left(right32_ref, right_ref, v, cscale * (2.0 * after - before))
    right_ref[...] = right32_ref[...].astype(jnp.bfloat16)

    forward_pass(rows_ref, cols_ref, live, held_ref, right_ref, stage_ref, out_ref)

    for r in range(ROWBLK):
        span = slice(r * EDGE, (r + 1) * EDGE)
        scale = rscale_ref[r : r + 1, :]
        y_out_ref[:, span] = jnp.maximum(
            0.0,
            y_ref[:, span]
            + step_size * ratio * (scale * (bound_ref[:, span] - joined(out_ref[r]))),
        )


def over_bands(value, combine):
    bands = lax.axis_size("band")
    hop = 1
    while hop < bands:
        other = lax.ppermute(value, "band", [(i, i ^ hop) for i in range(bands)])
        value = combine(value, other)
        hop *= 2
    return value


def shards(tiles, tile_row, tile_col, tile_count, cost, bound_vec, x_start, y_start):
    tiles = tiles[0]
    ntile = tiles.shape[0]
    bands = lax.axis_size("band")
    blocks = bands * COLBLK
    place = lax.axis_index("band").astype(jnp.int32).reshape(1)
    scalars = (place, tile_row[0], tile_col[0], tile_count)
    bound = bound_vec.reshape(1, -1)
    nrow = bound.shape[1]
    f32 = lambda *shape: jax.ShapeDtypeStruct(shape, jnp.float32)
    smem = [pl.BlockSpec(memory_space=pltpu.SMEM)] * 4
    hbm = [pl.BlockSpec(memory_space=pltpu.HBM)]
    vmem = lambda n: [pl.BlockSpec(memory_space=pltpu.VMEM)] * n
    left = [pltpu.VMEM((ROWBLK + 1, LEFT, EDGE), jnp.float32), pltpu.VMEM((ROWBLK + 1, LEFT, EDGE), jnp.bfloat16)]
    right = [pltpu.VMEM((blocks, LEFT, EDGE), jnp.float32), pltpu.VMEM((blocks, LEFT, EDGE), jnp.bfloat16)]
    rows_out = [pltpu.VMEM((ROWBLK + 1, KEPT, EDGE), jnp.float32)]
    sums = [pltpu.VMEM((blocks, KEPT, EDGE), jnp.float32)]
    stage = [pltpu.VMEM((2, GROUP, KEPT, EDGE), jnp.float32)]
    params = pltpu.CompilerParams(vmem_limit_bytes=32 * 1024 * 1024)

    send, rscale, held = pl.pallas_call(
        scale_kernel,
        out_shape=(f32(5 * blocks, EDGE), f32(ROWBLK, EDGE), pltpu.VMEM(tiles.shape, jnp.bfloat16)),
        in_specs=smem + hbm + vmem(3),
        out_specs=tuple(vmem(3)),
        scratch_shapes=[pltpu.SemaphoreType.DMA((ntile // GROUP,))]
        + [pltpu.VMEM((ROWBLK + 1, EDGE, EDGE), jnp.bfloat16), pltpu.VMEM((ROWBLK + 1, EDGE, EDGE), jnp.float32)]
        + left
        + [pltpu.VMEM((blocks, 8, EDGE), jnp.float32)]
        + stage
        + sums,
        compiler_params=params,
        name="scales",
    )(*scalars, pltpu.with_memory_space_constraint(tiles, pltpu.HBM), y_start, x_start, cost)

    is_peak = lax.broadcasted_iota(jnp.int32, send.shape, 0) < blocks
    got = over_bands(send, lambda a, b: jnp.where(is_peak, jnp.maximum(a, b), a + b))

    send, x_one, cscale, y_one, moved = pl.pallas_call(
        step_kernel,
        out_shape=(
            f32(VECS * blocks + 8, EDGE), f32(VECS * blocks, EDGE), f32(blocks, EDGE), f32(VECS, nrow), f32(VECS, EDGE),
        ),
        in_specs=smem + vmem(6),
        out_specs=tuple(vmem(5)),
        scratch_shapes=right + rows_out + left + stage + sums,
        compiler_params=params,
        name="first_step",
    )(*scalars, held, got, rscale, y_start, bound, cost)

    got = over_bands(send, lambda a, b: a + b)

    return pl.pallas_call(
        last_kernel,
        out_shape=(f32(*x_start.shape), f32(*y_start.shape)),
        in_specs=smem + vmem(8),
        out_specs=tuple(vmem(2)),
        scratch_shapes=right + stage + rows_out,
        compiler_params=params,
        name="second_step",
    )(*scalars, held, got, rscale, y_one, bound, x_one, cscale, moved)


def solution(mesh):
    return jax.shard_map(
        shards,
        mesh=mesh,
        in_specs=(
            P("band", None, None, None),
            P("band", None),
            P("band", None),
            P("band"),
            P("batch", "band"),
            P("band"),
            P("batch", "band"),
            P("batch", "band"),
        ),
        out_specs=(P("batch", "band"), P("batch", "band")),
        check_vma=False,
    )
```

```python
import functools

import jax
import jax.numpy as jnp
from jax import lax
from jax.experimental import pallas as pl
from jax.experimental.pallas import tpu as pltpu
from jax.sharding import PartitionSpec as P

ROWBLK = 4
COLBLK = 2
EDGE = 128
VECS = 4
TERMS = 2
KEPT = VECS * TERMS
LEFT = 16
FETCH = 16
GROUP = 32

step_size = 0.0625


def split(value):
    high = value.astype(jnp.bfloat16).astype(jnp.float32)
    return high, (value - high).astype(jnp.bfloat16).astype(jnp.float32)


def joined(rows):
    return rows[0:VECS] + rows[VECS : 2 * VECS]


def leads():
    return lax.axis_index("batch") % 2 == 1


def products(multiply, place, stage_ref, into_ref, ntile):
    stage_ref[1] = jnp.zeros(stage_ref.shape[1:], jnp.float32)

    def group(g, carry):
        now = g % 2
        for u in range(GROUP):
            stage_ref[now, u] = multiply(g * GROUP + u)[0:KEPT]
        for u in range(GROUP):
            into_ref[place(jnp.maximum((g - 1) * GROUP + u, 0))] += stage_ref[1 - now, u]
        return carry

    groups = ntile // GROUP
    lax.fori_loop(0, groups, group, 0)
    for u in range(GROUP):
        into_ref[place(ntile - GROUP + u)] += stage_ref[(groups - 1) % 2, u]


def put_left(left32_ref, left_ref, index, value):
    for s, term in enumerate(split(value)):
        left32_ref[index, VECS * s : VECS * (s + 1), :] = term
    left_ref[index] = left32_ref[index].astype(jnp.bfloat16)


def clear_left(left32_ref, left_ref):
    left32_ref[...] = jnp.zeros_like(left32_ref)
    left_ref[ROWBLK] = jnp.zeros((LEFT, EDGE), jnp.bfloat16)


def adjoint_start(sums_ref, costs, band):
    sums_ref[...] = jnp.zeros_like(sums_ref)
    for j in range(COLBLK):
        sums_ref[band * COLBLK + j, 0:VECS, :] = -costs[:, j * EDGE : (j + 1) * EDGE]


def adjoint_sum(sums_ref, v):
    blocks = sums_ref.shape[0]
    flat = sums_ref.reshape(blocks * KEPT, EDGE)
    return sum(flat[pl.ds(VECS * s + v, blocks, stride=KEPT), :] for s in range(TERMS))


def adjoint_pass(meta_ref, held_ref, left_ref, stage_ref, sums_ref):
    def multiply(t):
        return jnp.dot(left_ref[meta_ref[0, t]], held_ref[t], preferred_element_type=jnp.float32)

    products(multiply, lambda t: meta_ref[1, t], stage_ref, sums_ref, held_ref.shape[0])


def forward_left(right32_ref, v, value):
    blocks = right32_ref.shape[0]
    flat = right32_ref.reshape(blocks * LEFT, EDGE)
    for s, term in enumerate(split(value)):
        flat[pl.ds(VECS * s + v, blocks, stride=LEFT), :] = term


def forward_pass(meta_ref, turned_ref, right_ref, stage_ref, out_ref):
    def multiply(t):
        return jnp.dot(right_ref[meta_ref[1, t]], turned_ref[t], preferred_element_type=jnp.float32)

    out_ref[...] = jnp.zeros_like(out_ref)
    products(multiply, lambda t: meta_ref[0, t], stage_ref, out_ref, turned_ref.shape[0])


def scale_kernel(
    rows_ref, cols_ref, count_ref, tiles_ref, y_ref, x_ref, cost_ref,
    held_ref, meta_out_ref, spread_ref, rscale_ref, own_ref,
    sems, small_sems, rows_v_ref, rows_s_ref, count_s_ref, peak_ref,
):
    ntile = held_ref.shape[0]
    nrow, ncol = y_ref.shape[1], x_ref.shape[1]
    later = [
        pltpu.make_async_copy(y_ref, own_ref.at[:, 0:nrow], small_sems.at[4]),
        pltpu.make_async_copy(x_ref, own_ref.at[:, nrow : nrow + ncol], small_sems.at[5]),
        pltpu.make_async_copy(cost_ref, own_ref.at[:, nrow + ncol :], small_sems.at[6]),
    ]
    for copy in later:
        copy.start()

    def fetch(g):
        part = pl.ds(g * FETCH, FETCH)
        return pltpu.make_async_copy(tiles_ref.at[part], held_ref.at[part], sems.at[g])

    @pl.when(leads())
    def _():
        small = [
            pltpu.make_async_copy(rows_ref, rows_s_ref, small_sems.at[0]),
            pltpu.make_async_copy(rows_ref, rows_v_ref, small_sems.at[1]),
            pltpu.make_async_copy(cols_ref, meta_out_ref.at[1:2], small_sems.at[2]),
            pltpu.make_async_copy(count_ref, count_s_ref, small_sems.at[3]),
        ]
        for copy in small:
            copy.start()
        for g in range(ntile // FETCH):
            fetch(g).start()
        peak_ref[...] = jnp.zeros_like(peak_ref)
        spread_ref[ROWBLK] = jnp.zeros((EDGE, EDGE), jnp.float32)
        for copy in small:
            copy.wait()
        live = count_s_ref[0]
        index = lax.broadcasted_iota(jnp.int32, (1, ntile), 1)
        meta_out_ref[0:1, :] = jnp.where(index < live, rows_v_ref[...], ROWBLK)

        def row_peaks(g, carry):
            fetch(g).wait()
            for u in range(FETCH):
                t = g * FETCH + u
                r = jnp.where(t < live, rows_s_ref[0, t], ROWBLK)
                peak_ref[r] = jnp.maximum(peak_ref[r], jnp.abs(held_ref[t]))
            return carry

        lax.fori_loop(0, ntile // FETCH, row_peaks, 0)
        for r in range(ROWBLK):
            peak = jnp.max(peak_ref[r].astype(jnp.float32), axis=1, keepdims=True)
            spread = jnp.broadcast_to(lax.rsqrt(peak), (EDGE, EDGE))
            spread_ref[r] = spread
            rscale_ref[r : r + 1, :] = spread.T[0:1, :]

    for copy in later:
        copy.wait()


def columns_kernel(meta_ref, held_ref, spread_ref, top_out_ref, top_ref):
    @pl.when(leads())
    def _():
        top_ref[...] = jnp.zeros_like(top_ref)

        def group(g, carry):
            for u in range(FETCH):
                t = g * FETCH + u
                c = meta_ref[1, t]
                scaled = jnp.abs(held_ref[t]).astype(jnp.float32) * spread_ref[meta_ref[0, t]]
                peak = jnp.max(scaled.reshape(EDGE // 8, 8, EDGE), axis=0)
                top_ref[c] = jnp.maximum(top_ref[c], peak)
            return carry

        lax.fori_loop(0, held_ref.shape[0] // FETCH, group, 0)
        top_out_ref[...] = jnp.max(top_ref[...], axis=1)


def turn_kernel(held_ref, turned_ref):
    @pl.when(leads())
    def _():
        def group(g, carry):
            for u in range(FETCH):
                turned_ref[g * FETCH + u] = held_ref[g * FETCH + u].T
            return carry

        lax.fori_loop(0, held_ref.shape[0] // FETCH, group, 0)


def start_kernel(
    meta_ref, held_ref, rscale_ref, top_ref, mine_ref, other_ref,
    send_ref, both_ref,
    left32_ref, left_ref, stage_ref, sums_ref,
):
    blocks = sums_ref.shape[0]
    nrow = ROWBLK * EDGE
    ncol = COLBLK * EDGE

    @pl.when(leads())
    def _():
        both = jnp.concatenate([mine_ref[...], other_ref[...]], axis=0)
        both_ref[...] = both
        clear_left(left32_ref, left_ref)
        adjoint_start(sums_ref, both[:, nrow + ncol :], lax.axis_index("band"))
        for r in range(ROWBLK):
            put_left(
                left32_ref, left_ref, r, both[:, r * EDGE : (r + 1) * EDGE] * rscale_ref[r : r + 1, :]
            )
        send_ref[0:blocks, :] = top_ref[...]
        for j in range(COLBLK):
            at = (1 + VECS) * blocks + j * VECS
            send_ref[at : at + VECS, :] = both[:, nrow + j * EDGE : nrow + (j + 1) * EDGE]
        adjoint_pass(meta_ref, held_ref, left_ref, stage_ref, sums_ref)
        for v in range(VECS):
            send_ref[(1 + v) * blocks : (2 + v) * blocks, :] = adjoint_sum(sums_ref, v)


def combined(refs, blocks):
    peak = functools.reduce(jnp.maximum, [ref[0:blocks, :] for ref in refs])
    rows = slice(blocks, (1 + VECS) * blocks)
    return peak, functools.reduce(jnp.add, [ref[rows, :] for ref in refs])


def merge_kernel(blocks, *refs):
    refs, out_ref = refs[:-1], refs[-1]
    head = (1 + VECS) * blocks
    peak, total = combined(refs, blocks)
    out_ref[0:blocks, :] = peak
    out_ref[blocks:head, :] = total
    more = refs[0].shape[0] - head
    for i, ref in enumerate(refs):
        out_ref[head + i * more : head + (i + 1) * more, :] = ref[head:, :]


def step_kernel(
    offsets, parts, meta_ref, held_ref, turned_ref, *rest,
):
    got_refs = rest[:parts]
    (
        rscale_ref, both_ref, bound_ref,
        send_ref, x_one_ref, cscale_ref, y_one_ref, moved_ref,
        start_ref, right32_ref, right_ref, out_ref, left32_ref, left_ref, stage_ref, sums_ref,
    ) = rest[parts:]
    blocks = right_ref.shape[0]
    head = (1 + VECS) * blocks

    @pl.when(leads())
    def _():
        band = lax.axis_index("band")
        right32_ref[...] = jnp.zeros_like(right32_ref)
        clear_left(left32_ref, left_ref)
        adjoint_start(sums_ref, both_ref[:, (ROWBLK + COLBLK) * EDGE :], band)
        per = len(offsets) // parts
        for m, offset in enumerate(offsets):
            for j in range(COLBLK):
                at = head + (m % per) * COLBLK * VECS + j * VECS
                place = (band ^ offset) * COLBLK + j
                start_ref[place, 0:VECS, :] = got_refs[m // per][at : at + VECS, :]
        start = start_ref.reshape(blocks * 8, EDGE)

        peak, totals = combined(got_refs, blocks)
        cscale = lax.rsqrt(peak)
        cscale_ref[...] = cscale
        for v in range(VECS):
            before = start[pl.ds(v, blocks, stride=8), :]
            after = jnp.maximum(
                0.0, before + step_size * (cscale * totals[v * blocks : (v + 1) * blocks])
            )
            x_one_ref[v * blocks : (v + 1) * blocks, :] = after
            moved = jnp.sum(
                jnp.sum((after - before) ** 2, axis=0, keepdims=True), axis=1, keepdims=True
            )
            moved_ref[v : v + 1, :] = jnp.broadcast_to(moved, (1, EDGE))
            forward_left(right32_ref, v, cscale * (2.0 * after - before))
        right_ref[...] = right32_ref[...].astype(jnp.bfloat16)

        forward_pass(meta_ref, turned_ref, right_ref, stage_ref, out_ref)

        moved = jnp.zeros((VECS, EDGE), jnp.float32)
        for r in range(ROWBLK):
            span = slice(r * EDGE, (r + 1) * EDGE)
            scale = rscale_ref[r : r + 1, :]
            before = both_ref[:, span]
            after = jnp.maximum(
                0.0, before + step_size * (scale * (bound_ref[:, span] - joined(out_ref[r])))
            )
            y_one_ref[:, span] = after
            moved += (after - before) ** 2
            put_left(left32_ref, left_ref, r, after * scale)

        adjoint_pass(meta_ref, held_ref, left_ref, stage_ref, sums_ref)
        for v in range(VECS):
            send_ref[v * blocks : (v + 1) * blocks, :] = adjoint_sum(sums_ref, v)
        send_ref[VECS * blocks :, :] = jnp.zeros((8, EDGE), jnp.float32)
        send_ref[VECS * blocks : VECS * blocks + VECS, :] = moved


def last_kernel(parts, meta_ref, turned_ref, *rest):
    got_refs = rest[:parts]
    (
        rscale_ref, y_ref, bound_ref, x_one_ref, cscale_ref, moved_ref,
        mine_ref, other_ref,
        right32_ref, right_ref, out_ref, stage_ref,
    ) = rest[parts:]
    blocks = right_ref.shape[0]
    half = VECS // 2
    ncol = COLBLK * EDGE

    @pl.when(leads())
    def _():
        band = lax.axis_index("band")
        right32_ref[...] = jnp.zeros_like(right32_ref)
        cscale = cscale_ref[...]
        row = lax.broadcasted_iota(jnp.int32, (blocks, EDGE), 0)
        got = functools.reduce(jnp.add, [ref[...] for ref in got_refs])
        dual = jnp.sum(got[VECS * blocks : VECS * blocks + VECS], axis=1, keepdims=True)
        ratio = jnp.sqrt((dual + 1e-06) / (moved_ref[...] + 1e-06))
        for v in range(VECS):
            before = x_one_ref[v * blocks : (v + 1) * blocks, :]
            after = jnp.maximum(
                0.0,
                before
                + step_size / ratio[v : v + 1, :] * (cscale * got[v * blocks : (v + 1) * blocks]),
            )
            to_ref = mine_ref if v < half else other_ref
            for j in range(COLBLK):
                own = jnp.where(row == band * COLBLK + j, after, 0.0)
                to_ref[v % half : v % half + 1, j * EDGE : (j + 1) * EDGE] = jnp.sum(
                    own, axis=0, keepdims=True
                )
            forward_left(right32_ref, v, cscale * (2.0 * after - before))
        right_ref[...] = right32_ref[...].astype(jnp.bfloat16)

        forward_pass(meta_ref, turned_ref, right_ref, stage_ref, out_ref)

        for r in range(ROWBLK):
            span = slice(r * EDGE, (r + 1) * EDGE)
            scale = rscale_ref[r : r + 1, :]
            after = jnp.maximum(
                0.0,
                y_ref[:, span]
                + step_size * ratio * (scale * (bound_ref[:, span] - joined(out_ref[r]))),
            )
            place = slice(ncol + r * EDGE, ncol + (r + 1) * EDGE)
            mine_ref[:, place] = after[0:half]
            other_ref[:, place] = after[half:]


def finish_kernel(mine_ref, got_ref, x_ref, y_ref, sems):
    ncol = x_ref.shape[1]

    def give(from_ref):
        copies = [
            pltpu.make_async_copy(from_ref.at[:, 0:ncol], x_ref, sems.at[0]),
            pltpu.make_async_copy(from_ref.at[:, ncol:], y_ref, sems.at[1]),
        ]
        for copy in copies:
            copy.start()
        for copy in copies:
            copy.wait()

    pl.when(leads())(lambda: give(mine_ref))
    pl.when(jnp.logical_not(leads()))(lambda: give(got_ref))


def swap(value):
    count = lax.axis_size("batch")
    return lax.ppermute(value, "batch", [(i, i ^ 1) for i in range(count)])


def from_band(value, hop):
    bands, batches = lax.axis_size("band"), lax.axis_size("batch")
    pairs = []
    for band in range(bands):
        for batch in range(batches):
            if batch % 2 == 1:
                to = (band ^ hop) * batches + batch
            else:
                to = band * batches + (batch + 2) % batches if batches % 4 == 0 else (band ^ hop) * batches + batch
            pairs.append((band * batches + batch, to))
    return lax.ppermute(value, ("band", "batch"), pairs)


def rounds_of(bands):
    rounds, bit = [], 1
    while bit < bands:
        if bit * 2 < bands:
            rounds.append((bit, 2 * bit, 3 * bit))
        else:
            rounds.append((bit,))
        bit *= 4
    return rounds


def shards(tiles, tile_row, tile_col, tile_count, cost, bound_vec, x_start, y_start):
    tiles = tiles[0]
    ntile = tiles.shape[0]
    bands = lax.axis_size("band")
    blocks = bands * COLBLK
    bound = bound_vec.reshape(1, -1)
    nrow = bound.shape[1]
    f32 = lambda *shape: jax.ShapeDtypeStruct(shape, jnp.float32)
    v32 = lambda *shape: pltpu.VMEM(shape, jnp.float32)
    v16 = lambda *shape: pltpu.VMEM(shape, jnp.bfloat16)
    smem = [pl.BlockSpec(memory_space=pltpu.SMEM)]
    hbm = lambda n: [pl.BlockSpec(memory_space=pltpu.HBM)] * n
    vmem = lambda n: [pl.BlockSpec(memory_space=pltpu.VMEM)] * n
    left = [v32(ROWBLK + 1, LEFT, EDGE), v16(ROWBLK + 1, LEFT, EDGE)]
    right = [v32(blocks, LEFT, EDGE), v16(blocks, LEFT, EDGE)]
    rows_out = [v32(ROWBLK + 1, KEPT, EDGE)]
    sums = [v32(blocks, KEPT, EDGE)]
    stage = [v32(2, GROUP, KEPT, EDGE)]
    params = pltpu.CompilerParams(vmem_limit_bytes=32 * 1024 * 1024)
    in_hbm = lambda value: pltpu.with_memory_space_constraint(value, pltpu.HBM)

    held, meta, spread, rscale, mine = pl.pallas_call(
        scale_kernel,
        out_shape=(
            pltpu.VMEM(tiles.shape, jnp.bfloat16), pltpu.VMEM((2, ntile), jnp.int32),
            v32(ROWBLK + 1, EDGE, EDGE), v32(ROWBLK, EDGE),
            v32(y_start.shape[0], nrow + 2 * COLBLK * EDGE),
        ),
        in_specs=hbm(2) + [pl.BlockSpec(memory_space=pl.ANY)] + hbm(4),
        out_specs=tuple(vmem(5)),
        scratch_shapes=[
            pltpu.SemaphoreType.DMA((ntile // FETCH,)),
            pltpu.SemaphoreType.DMA((7,)),
            pltpu.VMEM((1, ntile), jnp.int32),
            pltpu.SMEM((1, ntile), jnp.int32),
            pltpu.SMEM((1,), jnp.int32),
            v16(ROWBLK + 1, EDGE, EDGE),
        ],
        compiler_params=params,
        name="row_scales",
    )(in_hbm(tile_row), in_hbm(tile_col), tile_count, *map(in_hbm, (tiles, y_start, x_start, cost)))

    other = swap(mine)

    top = pl.pallas_call(
        columns_kernel,
        out_shape=v32(blocks, EDGE),
        in_specs=smem + vmem(2),
        out_specs=vmem(1)[0],
        scratch_shapes=[v32(blocks, 8, EDGE)],
        compiler_params=params,
        cost_estimate=pl.CostEstimate(flops=0, bytes_accessed=tiles.nbytes, transcendentals=0),
        name="columns",
    )(meta, held, spread)

    turned = pl.pallas_call(
        turn_kernel,
        out_shape=v16(*tiles.shape),
        in_specs=vmem(1),
        out_specs=vmem(1)[0],
        compiler_params=params,
        cost_estimate=pl.CostEstimate(flops=0, bytes_accessed=tiles.nbytes, transcendentals=0),
        name="turn",
    )(held)

    message, both = pl.pallas_call(
        start_kernel,
        out_shape=(f32((1 + VECS) * blocks + COLBLK * VECS, EDGE), v32(VECS, mine.shape[1])),
        in_specs=smem + vmem(5),
        out_specs=tuple(vmem(2)),
        scratch_shapes=left + stage + sums,
        compiler_params=params,
        name="start",
    )(meta, held, rscale, top, mine, other)

    rounds = rounds_of(bands)
    offsets = [0]
    for index, hops in enumerate(rounds):
        messages = [message] + [from_band(message, hop) for hop in hops]
        offsets = [hop ^ offset for hop in (0, *hops) for offset in offsets]
        if index < len(rounds) - 1:
            message = pl.pallas_call(
                functools.partial(merge_kernel, blocks),
                out_shape=f32((1 + VECS) * blocks + COLBLK * VECS * len(offsets), EDGE),
                in_specs=vmem(len(messages)),
                out_specs=vmem(1)[0],
                compiler_params=params,
                name="merge",
            )(*messages)

    message, x_one, cscale, y_one, moved = pl.pallas_call(
        functools.partial(step_kernel, offsets, len(messages)),
        out_shape=(
            f32(VECS * blocks + 8, EDGE), v32(VECS * blocks, EDGE), v32(blocks, EDGE), v32(VECS, nrow), v32(VECS, EDGE),
        ),
        in_specs=smem + vmem(5 + len(messages)),
        out_specs=tuple(vmem(5)),
        scratch_shapes=[v32(blocks, 8, EDGE)] + right + rows_out + left + stage + sums,
        compiler_params=params,
        name="first_step",
    )(meta, held, turned, *messages, rscale, both, bound)

    for index, hops in enumerate(rounds):
        messages = [message] + [from_band(message, hop) for hop in hops]
        if index < len(rounds) - 1:
            message = functools.reduce(jnp.add, messages)

    half = VECS // 2
    width = COLBLK * EDGE + nrow
    mine, other = pl.pallas_call(
        functools.partial(last_kernel, len(messages)),
        out_shape=(v32(half, width), v32(half, width)),
        in_specs=smem + vmem(7 + len(messages)),
        out_specs=tuple(vmem(2)),
        scratch_shapes=right + rows_out + stage,
        compiler_params=params,
        name="second_step",
    )(meta, turned, *messages, rscale, y_one, bound, x_one, cscale, moved)

    return pl.pallas_call(
        finish_kernel,
        out_shape=(f32(*x_start.shape), f32(*y_start.shape)),
        in_specs=vmem(2),
        out_specs=tuple(hbm(2)),
        scratch_shapes=[pltpu.SemaphoreType.DMA((2,))],
        compiler_params=params,
        name="finish",
    )(mine, pltpu.with_memory_space_constraint(swap(other), pltpu.VMEM))


def solution(mesh):
    return jax.shard_map(
        shards,
        mesh=mesh,
        in_specs=(
            P("band", None, None, None),
            P("band", None),
            P("band", None),
            P("band"),
            P("batch", "band"),
            P("band"),
            P("batch", "band"),
            P("batch", "band"),
        ),
        out_specs=(P("batch", "band"), P("batch", "band")),
        check_vma=False,
    )
```

```python
import functools

import jax
import jax.numpy as jnp
from jax import lax
from jax.experimental import pallas as pl
from jax.experimental.pallas import tpu as pltpu
from jax.sharding import PartitionSpec as P

ROWBLK = 4
COLBLK = 2
EDGE = 128
VECS = 4
TERMS = 2
KEPT = VECS * TERMS
FETCH = 16

step_size = 0.0625


def split(value):
    high = value.astype(jnp.bfloat16).astype(jnp.float32)
    return high, (value - high).astype(jnp.bfloat16).astype(jnp.float32)


def joined(rows):
    return rows[0:VECS] + rows[VECS : 2 * VECS]


def leads():
    return lax.axis_index("batch") % 2 == 1


def pair_blocks(ref, index, rows):
    count = ref.shape[0] // 2
    empty = jnp.zeros_like(rows)
    ref[index] = jnp.concatenate([rows, empty], axis=0).astype(jnp.bfloat16)
    ref[count + index] = jnp.concatenate([empty, rows], axis=0).astype(jnp.bfloat16)


def put_left(left_ref, index, value):
    pair_blocks(left_ref, index, jnp.concatenate(split(value), axis=0))


def clear_left(left_ref):
    pair_blocks(left_ref, ROWBLK, jnp.zeros((KEPT, EDGE), jnp.float32))


def adjoint_start(sums_refs, costs, band):
    for ref in sums_refs:
        ref[...] = jnp.zeros_like(ref)
    for j in range(COLBLK):
        sums_refs[0][band * COLBLK + j, 0:VECS, :] = -costs[:, j * EDGE : (j + 1) * EDGE]


def adjoint_sum(sums_refs, v):
    blocks = sums_refs[0].shape[0]
    total = 0.0
    for ref in sums_refs:
        flat = ref.reshape(blocks * KEPT, EDGE)
        for s in range(TERMS):
            total += flat[pl.ds(VECS * s + v, blocks, stride=KEPT), :]
    return total


def forward_left(right32_ref, v, value):
    blocks = right32_ref.shape[0]
    flat = right32_ref.reshape(blocks * KEPT, EDGE)
    for s, term in enumerate(split(value)):
        flat[pl.ds(VECS * s + v, blocks, stride=KEPT), :] = term


def tile_pass(meta_ref, tiles_refs, left_ref, of_row, into_refs, each=None):
    count = left_ref.shape[0] // 2
    first = 0
    for tiles_ref in tiles_refs:
        ntile = tiles_ref.shape[0]
        for t in range(0, ntile, 2):
            rows = [meta_ref[0, first + t], meta_ref[0, first + t + 1]]
            cols = [meta_ref[1, first + t], meta_ref[1, first + t + 1]]
            source, place = (rows, cols) if of_row else (cols, rows)
            left = jnp.concatenate([left_ref[source[0]], left_ref[count + source[1]]], axis=1)
            pair = tiles_ref[t : t + 2].reshape(2 * EDGE, EDGE)
            product = jnp.dot(left, pair, preferred_element_type=jnp.float32)
            for u in range(2):
                part = product[u * KEPT : (u + 1) * KEPT]
                into_refs[u][place[u]] += jnp.where(rows[u] < ROWBLK, part, 0.0)
                if each is not None:
                    each(tiles_ref[t + u], rows[u], cols[u], u)
        first += ntile


def fetch(tiles_ref, held_ref, sems, first, g):
    from_part, to_part = pl.ds(g * FETCH, FETCH), pl.ds((g - first) * FETCH, FETCH)
    return pltpu.make_async_copy(tiles_ref.at[from_part], held_ref.at[to_part], sems.at[g - first])


def row_peaks(row_at, held_ref, peak_refs, first, g):
    for u in range(FETCH):
        t = g * FETCH + u
        r = row_at(t)
        ref = peak_refs[u % 2]
        ref[r] = jnp.maximum(ref[r], jnp.abs(held_ref[t - first * FETCH]))


def pack_kernel(
    rows_ref, cols_ref, y_ref, x_ref, cost_ref, tiles_ref,
    meta_ref, own_ref, held_ref, even_ref, odd_ref,
    small_sems, sems, rows_s_ref,
):
    nrow, ncol = y_ref.shape[1], x_ref.shape[1]
    groups = held_ref.shape[0] // FETCH
    copies = [
        pltpu.make_async_copy(rows_ref, rows_s_ref, small_sems.at[0]),
        pltpu.make_async_copy(rows_ref, meta_ref.at[0:1], small_sems.at[1]),
        pltpu.make_async_copy(cols_ref, meta_ref.at[1:2], small_sems.at[2]),
        pltpu.make_async_copy(y_ref, own_ref.at[:, 0:nrow], small_sems.at[3]),
        pltpu.make_async_copy(x_ref, own_ref.at[:, nrow : nrow + ncol], small_sems.at[4]),
        pltpu.make_async_copy(cost_ref, own_ref.at[:, nrow + ncol :], small_sems.at[5]),
    ]
    for copy in copies:
        copy.start()

    @pl.when(leads())
    def _():
        for g in range(groups):
            fetch(tiles_ref, held_ref, sems, 0, g).start()
        for ref in (even_ref, odd_ref):
            ref[...] = jnp.zeros_like(ref)

    for copy in copies:
        copy.wait()

    @pl.when(leads())
    def _():
        def group(g, carry):
            fetch(tiles_ref, held_ref, sems, 0, g).wait()
            row_peaks(lambda t: rows_s_ref[0, t], held_ref, (even_ref, odd_ref), 0, g)
            return carry

        lax.fori_loop(0, groups, group, 0)


def scale_kernel(
    meta_ref, count_ref, even_in_ref, odd_in_ref, tiles_ref,
    meta_out_ref, held_ref, spread_ref, rscale_ref,
    meta_sem, sems, meta_s_ref, even_ref, odd_ref,
):
    groups = tiles_ref.shape[0] // FETCH
    first = groups - held_ref.shape[0] // FETCH

    @pl.when(leads())
    def _():
        for g in range(first, groups):
            fetch(tiles_ref, held_ref, sems, first, g).start()
        index = lax.broadcasted_iota(jnp.int32, (1, tiles_ref.shape[0]), 1)
        meta_out_ref[0:1, :] = jnp.where(index < count_ref[...], meta_ref[0:1, :], ROWBLK)
        meta_out_ref[1:2, :] = meta_ref[1:2, :]
        copy = pltpu.make_async_copy(meta_out_ref, meta_s_ref, meta_sem)
        copy.start()
        even_ref[...] = even_in_ref[...]
        odd_ref[...] = odd_in_ref[...]
        spread_ref[ROWBLK] = jnp.zeros((EDGE, EDGE), jnp.float32)
        copy.wait()

        def group(g, carry):
            fetch(tiles_ref, held_ref, sems, first, g).wait()
            row_peaks(lambda t: meta_s_ref[0, t], held_ref, (even_ref, odd_ref), first, g)
            return carry

        lax.fori_loop(first, groups, group, 0)
        for r in range(ROWBLK):
            peak = jnp.maximum(even_ref[r], odd_ref[r]).astype(jnp.float32)
            scale = lax.rsqrt(jnp.max(peak, axis=1, keepdims=True))
            spread_ref[r] = jnp.broadcast_to(scale, (EDGE, EDGE))
            rscale_ref[r : r + 1, :] = lax.rsqrt(jnp.max(peak.T, axis=0, keepdims=True))


def turn_kernel(one_ref, two_ref, turned_ref):
    @pl.when(leads())
    def _():
        first = 0
        for ref in (one_ref, two_ref):
            for t in range(ref.shape[0]):
                turned_ref[first + t] = ref[t].T
            first += ref.shape[0]


def start_kernel(
    meta_ref, one_ref, two_ref, spread_ref, rscale_ref, mine_ref, other_ref,
    send_ref, both_ref,
    left_ref, top_ref, top_two_ref, sums_ref, sums_two_ref,
):
    blocks = sums_ref.shape[0]
    sums_refs = (sums_ref, sums_two_ref)
    top_refs = (top_ref, top_two_ref)
    nrow = ROWBLK * EDGE
    ncol = COLBLK * EDGE

    @pl.when(leads())
    def _():
        both = jnp.concatenate([mine_ref[...], other_ref[...]], axis=0)
        both_ref[...] = both
        for ref in top_refs:
            ref[...] = jnp.zeros_like(ref)
        clear_left(left_ref)
        adjoint_start(sums_refs, both[:, nrow + ncol :], lax.axis_index("band"))
        for r in range(ROWBLK):
            put_left(left_ref, r, both[:, r * EDGE : (r + 1) * EDGE] * rscale_ref[r : r + 1, :])
        for j in range(COLBLK):
            at = (1 + VECS) * blocks + j * VECS
            send_ref[at : at + VECS, :] = both[:, nrow + j * EDGE : nrow + (j + 1) * EDGE]

        def column_peaks(tile, r, c, u):
            scaled = jnp.abs(tile).astype(jnp.float32) * spread_ref[r]
            peak = jnp.max(scaled.reshape(EDGE // 8, 8, EDGE), axis=0)
            top_refs[u][c] = jnp.maximum(top_refs[u][c], peak)

        tile_pass(meta_ref, (one_ref, two_ref), left_ref, True, sums_refs, column_peaks)
        send_ref[0:blocks, :] = jnp.max(jnp.maximum(top_ref[...], top_two_ref[...]), axis=1)
        for v in range(VECS):
            send_ref[(1 + v) * blocks : (2 + v) * blocks, :] = adjoint_sum(sums_refs, v)


def combined(refs, blocks):
    peak = functools.reduce(jnp.maximum, [ref[0:blocks, :] for ref in refs])
    rows = slice(blocks, (1 + VECS) * blocks)
    return peak, functools.reduce(jnp.add, [ref[rows, :] for ref in refs])


def merge_kernel(blocks, *refs):
    refs, out_ref = refs[:-1], refs[-1]
    head = (1 + VECS) * blocks
    peak, total = combined(refs, blocks)
    out_ref[0:blocks, :] = peak
    out_ref[blocks:head, :] = total
    more = refs[0].shape[0] - head
    for i, ref in enumerate(refs):
        out_ref[head + i * more : head + (i + 1) * more, :] = ref[head:, :]


def step_kernel(
    offsets, parts, meta_ref, one_ref, two_ref, turned_ref, *rest,
):
    got_refs = rest[:parts]
    (
        rscale_ref, both_ref, bound_ref,
        send_ref, x_one_ref, cscale_ref, y_one_ref, moved_ref,
        start_ref, right32_ref, right_ref, out_ref, out_two_ref, left_ref, sums_ref, sums_two_ref,
    ) = rest[parts:]
    blocks = right32_ref.shape[0]
    head = (1 + VECS) * blocks
    sums_refs = (sums_ref, sums_two_ref)

    @pl.when(leads())
    def _():
        band = lax.axis_index("band")
        clear_left(left_ref)
        adjoint_start(sums_refs, both_ref[:, (ROWBLK + COLBLK) * EDGE :], band)
        per = len(offsets) // parts
        for m, offset in enumerate(offsets):
            for j in range(COLBLK):
                at = head + (m % per) * COLBLK * VECS + j * VECS
                place = (band ^ offset) * COLBLK + j
                start_ref[place, 0:VECS, :] = got_refs[m // per][at : at + VECS, :]
        start = start_ref.reshape(blocks * 8, EDGE)

        peak, totals = combined(got_refs, blocks)
        cscale = lax.rsqrt(peak)
        cscale_ref[...] = cscale
        for v in range(VECS):
            before = start[pl.ds(v, blocks, stride=8), :]
            after = jnp.maximum(
                0.0, before + step_size * (cscale * totals[v * blocks : (v + 1) * blocks])
            )
            x_one_ref[v * blocks : (v + 1) * blocks, :] = after
            moved = jnp.sum(
                jnp.sum((after - before) ** 2, axis=0, keepdims=True), axis=1, keepdims=True
            )
            moved_ref[v : v + 1, :] = jnp.broadcast_to(moved, (1, EDGE))
            forward_left(right32_ref, v, cscale * (2.0 * after - before))
        for c in range(blocks):
            pair_blocks(right_ref, c, right32_ref[c])

        for ref in (out_ref, out_two_ref):
            ref[...] = jnp.zeros_like(ref)
        tile_pass(meta_ref, (turned_ref,), right_ref, False, (out_ref, out_two_ref))

        moved = jnp.zeros((VECS, EDGE), jnp.float32)
        for r in range(ROWBLK):
            span = slice(r * EDGE, (r + 1) * EDGE)
            scale = rscale_ref[r : r + 1, :]
            before = both_ref[:, span]
            after = jnp.maximum(
                0.0, before + step_size * (scale * (bound_ref[:, span] - joined(out_ref[r] + out_two_ref[r])))
            )
            y_one_ref[:, span] = after
            moved += (after - before) ** 2
            put_left(left_ref, r, after * scale)

        tile_pass(meta_ref, (one_ref, two_ref), left_ref, True, sums_refs)
        for v in range(VECS):
            send_ref[v * blocks : (v + 1) * blocks, :] = adjoint_sum(sums_refs, v)
        send_ref[VECS * blocks :, :] = jnp.zeros((8, EDGE), jnp.float32)
        send_ref[VECS * blocks : VECS * blocks + VECS, :] = moved


def last_kernel(parts, meta_ref, turned_ref, *rest):
    got_refs = rest[:parts]
    (
        rscale_ref, y_ref, bound_ref, x_one_ref, cscale_ref, moved_ref,
        mine_ref, other_ref,
        right32_ref, right_ref, out_ref, out_two_ref,
    ) = rest[parts:]
    blocks = right32_ref.shape[0]
    half = VECS // 2
    ncol = COLBLK * EDGE

    @pl.when(leads())
    def _():
        band = lax.axis_index("band")
        cscale = cscale_ref[...]
        row = lax.broadcasted_iota(jnp.int32, (blocks, EDGE), 0)
        got = functools.reduce(jnp.add, [ref[...] for ref in got_refs])
        dual = jnp.sum(got[VECS * blocks : VECS * blocks + VECS], axis=1, keepdims=True)
        ratio = jnp.sqrt((dual + 1e-06) / (moved_ref[...] + 1e-06))
        for v in range(VECS):
            before = x_one_ref[v * blocks : (v + 1) * blocks, :]
            after = jnp.maximum(
                0.0,
                before
                + step_size / ratio[v : v + 1, :] * (cscale * got[v * blocks : (v + 1) * blocks]),
            )
            to_ref = mine_ref if v < half else other_ref
            for j in range(COLBLK):
                own = jnp.where(row == band * COLBLK + j, after, 0.0)
                to_ref[v % half : v % half + 1, j * EDGE : (j + 1) * EDGE] = jnp.sum(
                    own, axis=0, keepdims=True
                )
            forward_left(right32_ref, v, cscale * (2.0 * after - before))
        for c in range(blocks):
            pair_blocks(right_ref, c, right32_ref[c])

        for ref in (out_ref, out_two_ref):
            ref[...] = jnp.zeros_like(ref)
        tile_pass(meta_ref, (turned_ref,), right_ref, False, (out_ref, out_two_ref))

        for r in range(ROWBLK):
            span = slice(r * EDGE, (r + 1) * EDGE)
            scale = rscale_ref[r : r + 1, :]
            after = jnp.maximum(
                0.0,
                y_ref[:, span]
                + step_size * ratio * (scale * (bound_ref[:, span] - joined(out_ref[r] + out_two_ref[r]))),
            )
            place = slice(ncol + r * EDGE, ncol + (r + 1) * EDGE)
            mine_ref[:, place] = after[0:half]
            other_ref[:, place] = after[half:]


def finish_kernel(mine_ref, got_ref, x_ref, y_ref, sems):
    ncol = x_ref.shape[1]

    def give(from_ref):
        copies = [
            pltpu.make_async_copy(from_ref.at[:, 0:ncol], x_ref, sems.at[0]),
            pltpu.make_async_copy(from_ref.at[:, ncol:], y_ref, sems.at[1]),
        ]
        for copy in copies:
            copy.start()
        for copy in copies:
            copy.wait()

    pl.when(leads())(lambda: give(mine_ref))
    pl.when(jnp.logical_not(leads()))(lambda: give(got_ref))


def swap(value):
    count = lax.axis_size("batch")
    return lax.ppermute(value, "batch", [(i, i ^ 1) for i in range(count)])


def from_band(value, hop):
    bands, batches = lax.axis_size("band"), lax.axis_size("batch")
    pairs = []
    for band in range(bands):
        for batch in range(batches):
            if batch % 2 == 1:
                to = (band ^ hop) * batches + batch
            else:
                to = band * batches + (batch + 2) % batches if batches % 4 == 0 else (band ^ hop) * batches + batch
            pairs.append((band * batches + batch, to))
    return lax.ppermute(value, ("band", "batch"), pairs)


def rounds_of(bands):
    rounds, bit = [], 1
    while bit < bands:
        if bit * 2 < bands:
            rounds.append((bit, 2 * bit, 3 * bit))
        else:
            rounds.append((bit,))
        bit *= 4
    return rounds


def shards(tiles, tile_row, tile_col, tile_count, cost, bound_vec, x_start, y_start):
    tiles = tiles[0]
    ntile = tiles.shape[0]
    bands = lax.axis_size("band")
    blocks = bands * COLBLK
    bound = bound_vec.reshape(1, -1)
    nrow = bound.shape[1]
    f32 = lambda *shape: jax.ShapeDtypeStruct(shape, jnp.float32)
    v32 = lambda *shape: pltpu.VMEM(shape, jnp.float32)
    v16 = lambda *shape: pltpu.VMEM(shape, jnp.bfloat16)
    smem = [pl.BlockSpec(memory_space=pltpu.SMEM)]
    hbm = lambda n: [pl.BlockSpec(memory_space=pltpu.HBM)] * n
    vmem = lambda n: [pl.BlockSpec(memory_space=pltpu.VMEM)] * n
    left = [v16(2 * (ROWBLK + 1), 2 * KEPT, EDGE)]
    right = [v32(blocks, KEPT, EDGE), v16(2 * blocks, 2 * KEPT, EDGE)]
    rows_out = [v32(ROWBLK + 1, KEPT, EDGE)] * 2
    sums = [v32(blocks, KEPT, EDGE)] * 2
    params = pltpu.CompilerParams(vmem_limit_bytes=32 * 1024 * 1024)
    in_hbm = lambda value: pltpu.with_memory_space_constraint(value, pltpu.HBM)

    early = ntile * 3 // 8
    small = (tile_row, tile_col, y_start, x_start, cost)
    peaks = [v16(ROWBLK + 1, EDGE, EDGE)] * 2
    tiles = in_hbm(tiles)
    meta, mine, one, *tops = pl.pallas_call(
        pack_kernel,
        out_shape=(
            pltpu.VMEM((2, ntile), jnp.int32), v32(VECS // 2, nrow + 2 * COLBLK * EDGE), v16(early, EDGE, EDGE), *peaks,
        ),
        in_specs=hbm(6),
        out_specs=tuple(vmem(5)),
        scratch_shapes=[
            pltpu.SemaphoreType.DMA((6,)),
            pltpu.SemaphoreType.DMA((early // FETCH,)),
            pltpu.SMEM((1, ntile), jnp.int32),
        ],
        compiler_params=params,
        name="pack",
    )(*map(in_hbm, small), tiles)
    other = swap(mine)

    late = ntile - early
    meta, two, spread, rscale = pl.pallas_call(
        scale_kernel,
        out_shape=(
            pltpu.VMEM((2, ntile), jnp.int32), v16(late, EDGE, EDGE), v32(ROWBLK + 1, EDGE, EDGE), v32(ROWBLK, EDGE),
        ),
        in_specs=vmem(4) + hbm(1),
        out_specs=tuple(vmem(4)),
        scratch_shapes=[
            pltpu.SemaphoreType.DMA,
            pltpu.SemaphoreType.DMA((late // FETCH,)),
            pltpu.SMEM((2, ntile), jnp.int32),
            *peaks,
        ],
        compiler_params=params,
        cost_estimate=pl.CostEstimate(flops=0, bytes_accessed=tiles.nbytes, transcendentals=0),
        name="row_scales",
    )(meta, tile_count.reshape(1, 1), *tops, tiles)

    turned = pl.pallas_call(
        turn_kernel,
        out_shape=v16(*tiles.shape),
        in_specs=vmem(2),
        out_specs=vmem(1)[0],
        compiler_params=params,
        cost_estimate=pl.CostEstimate(flops=0, bytes_accessed=tiles.nbytes, transcendentals=0),
        name="turn",
    )(one, two)

    message, both = pl.pallas_call(
        start_kernel,
        out_shape=(f32((1 + VECS) * blocks + COLBLK * VECS, EDGE), v32(VECS, mine.shape[1])),
        in_specs=smem + vmem(6),
        out_specs=tuple(vmem(2)),
        scratch_shapes=left + [v32(blocks, 8, EDGE)] * 2 + sums,
        compiler_params=params,
        name="start",
    )(meta, one, two, spread, rscale, mine, other)

    rounds = rounds_of(bands)
    offsets = [0]
    for index, hops in enumerate(rounds):
        messages = [message] + [from_band(message, hop) for hop in hops]
        offsets = [hop ^ offset for hop in (0, *hops) for offset in offsets]
        if index < len(rounds) - 1:
            message = pl.pallas_call(
                functools.partial(merge_kernel, blocks),
                out_shape=f32((1 + VECS) * blocks + COLBLK * VECS * len(offsets), EDGE),
                in_specs=vmem(len(messages)),
                out_specs=vmem(1)[0],
                compiler_params=params,
                name="merge",
            )(*messages)

    message, x_one, cscale, y_one, moved = pl.pallas_call(
        functools.partial(step_kernel, offsets, len(messages)),
        out_shape=(
            f32(VECS * blocks + 8, EDGE), v32(VECS * blocks, EDGE), v32(blocks, EDGE), v32(VECS, nrow), v32(VECS, EDGE),
        ),
        in_specs=smem + vmem(6 + len(messages)),
        out_specs=tuple(vmem(5)),
        scratch_shapes=[v32(blocks, 8, EDGE)] + right + rows_out + left + sums,
        compiler_params=params,
        name="first_step",
    )(meta, one, two, turned, *messages, rscale, both, bound)

    for index, hops in enumerate(rounds):
        messages = [message] + [from_band(message, hop) for hop in hops]
        if index < len(rounds) - 1:
            message = functools.reduce(jnp.add, messages)

    half = VECS // 2
    width = COLBLK * EDGE + nrow
    mine, other = pl.pallas_call(
        functools.partial(last_kernel, len(messages)),
        out_shape=(v32(half, width), v32(half, width)),
        in_specs=smem + vmem(7 + len(messages)),
        out_specs=tuple(vmem(2)),
        scratch_shapes=right + rows_out,
        compiler_params=params,
        name="second_step",
    )(meta, turned, *messages, rscale, y_one, bound, x_one, cscale, moved)

    return pl.pallas_call(
        finish_kernel,
        out_shape=(f32(*x_start.shape), f32(*y_start.shape)),
        in_specs=vmem(2),
        out_specs=tuple(hbm(2)),
        scratch_shapes=[pltpu.SemaphoreType.DMA((2,))],
        compiler_params=params,
        name="finish",
    )(mine, pltpu.with_memory_space_constraint(swap(other), pltpu.VMEM))


def solution(mesh):
    return jax.shard_map(
        shards,
        mesh=mesh,
        in_specs=(
            P("band", None, None, None),
            P("band", None),
            P("band", None),
            P("band"),
            P("batch", "band"),
            P("band"),
            P("batch", "band"),
            P("batch", "band"),
        ),
        out_specs=(P("batch", "band"), P("batch", "band")),
        check_vma=False,
    )
```

```python
import functools

import jax
import jax.numpy as jnp
from jax import lax
from jax.experimental import pallas as pl
from jax.experimental.pallas import tpu as pltpu
from jax.sharding import PartitionSpec as P

ROWBLK = 4
COLBLK = 2
EDGE = 128
VECS = 4
TERMS = 2
KEPT = VECS * TERMS
FETCH = 16

step_size = 0.0625


def split(value):
    high = value.astype(jnp.bfloat16).astype(jnp.float32)
    return high, (value - high).astype(jnp.bfloat16).astype(jnp.float32)


def joined(rows):
    return rows[0:VECS] + rows[VECS : 2 * VECS]


def leads():
    return lax.axis_index("batch") % 2 == 1


def pair_blocks(ref, index, rows):
    count = ref.shape[0] // 2
    empty = jnp.zeros_like(rows)
    ref[index] = jnp.concatenate([rows, empty], axis=0).astype(jnp.bfloat16)
    ref[count + index] = jnp.concatenate([empty, rows], axis=0).astype(jnp.bfloat16)


def put_left(left_ref, index, value):
    pair_blocks(left_ref, index, jnp.concatenate(split(value), axis=0))


def clear_left(left_ref):
    pair_blocks(left_ref, ROWBLK, jnp.zeros((KEPT, EDGE), jnp.float32))


def adjoint_start(sums_refs, costs, band):
    for ref in sums_refs:
        ref[...] = jnp.zeros_like(ref)
    for j in range(COLBLK):
        sums_refs[0][band * COLBLK + j, 0:VECS, :] = -costs[:, j * EDGE : (j + 1) * EDGE]


def adjoint_sum(sums_refs, v):
    blocks = sums_refs[0].shape[0]
    total = 0.0
    for ref in sums_refs:
        flat = ref.reshape(blocks * KEPT, EDGE)
        for s in range(TERMS):
            total += flat[pl.ds(VECS * s + v, blocks, stride=KEPT), :]
    return total


def forward_left(right32_ref, v, value):
    blocks = right32_ref.shape[0]
    flat = right32_ref.reshape(blocks * KEPT, EDGE)
    for s, term in enumerate(split(value)):
        flat[pl.ds(VECS * s + v, blocks, stride=KEPT), :] = term


def row_of(meta_ref, count_ref, t):
    return jnp.where(t < count_ref[0], meta_ref[0, t], ROWBLK)


def tile_pass(meta_ref, count_ref, tiles_ref, left_ref, of_row, into_refs):
    count = left_ref.shape[0] // 2
    for t in range(0, tiles_ref.shape[0], 2):
        rows = [row_of(meta_ref, count_ref, t + u) for u in range(2)]
        cols = [meta_ref[1, t + u] for u in range(2)]
        source, place = (rows, cols) if of_row else (cols, rows)
        left = jnp.concatenate([left_ref[source[0]], left_ref[count + source[1]]], axis=1)
        pair = tiles_ref[t : t + 2].reshape(2 * EDGE, EDGE)
        product = jnp.dot(left, pair, preferred_element_type=jnp.float32)
        for u in range(2):
            part = product[u * KEPT : (u + 1) * KEPT]
            into_refs[u][place[u]] += jnp.where(rows[u] < ROWBLK, part, 0.0)


def scale_kernel(
    rows_ref, cols_ref, count_ref, y_ref, x_ref, cost_ref, tiles_ref,
    meta_ref, own_ref, held_ref, spread_ref, rscale_ref,
    small_sems, sems, even_ref, odd_ref,
):
    nrow, ncol = y_ref.shape[1], x_ref.shape[1]
    parts = sems.shape[0]
    per = held_ref.shape[0] // parts
    places = [
        pltpu.make_async_copy(rows_ref, meta_ref.at[0:1], small_sems.at[0]),
        pltpu.make_async_copy(cols_ref, meta_ref.at[1:2], small_sems.at[1]),
    ]
    vectors = [
        pltpu.make_async_copy(y_ref, own_ref.at[:, 0:nrow], small_sems.at[2]),
        pltpu.make_async_copy(x_ref, own_ref.at[:, nrow : nrow + ncol], small_sems.at[3]),
        pltpu.make_async_copy(cost_ref, own_ref.at[:, nrow + ncol :], small_sems.at[4]),
    ]
    for copy in places:
        copy.start()

    @pl.when(leads())
    def _():
        peak_refs = (even_ref, odd_ref)
        fetches = []
        for g in range(parts):
            part = pl.ds(g * per, per)
            fetches.append(pltpu.make_async_copy(tiles_ref.at[part], held_ref.at[part], sems.at[g]))
            fetches[g].start()
        for copy in vectors:
            copy.start()
        for ref in peak_refs:
            ref[...] = jnp.zeros_like(ref)
        spread_ref[ROWBLK] = jnp.zeros((EDGE, EDGE), jnp.float32)
        for copy in places:
            copy.wait()
        for t in range(held_ref.shape[0]):
            if t % per == 0:
                fetches[t // per].wait()
            r = row_of(meta_ref, count_ref, t)
            tile = held_ref[t]
            ref = peak_refs[t % 2]
            ref[r] = jnp.maximum(ref[r], jnp.maximum(tile, -tile))
        for r in range(ROWBLK):
            peak = jnp.maximum(even_ref[r], odd_ref[r]).astype(jnp.float32)
            scale = lax.rsqrt(jnp.max(peak, axis=1, keepdims=True))
            spread_ref[r] = jnp.broadcast_to(scale, (EDGE, EDGE))
            rscale_ref[r : r + 1, :] = lax.rsqrt(jnp.max(peak.T, axis=0, keepdims=True))
        for copy in vectors:
            copy.wait()

    @pl.when(jnp.logical_not(leads()))
    def _():
        for copy in vectors:
            copy.start()
        for copy in places + vectors:
            copy.wait()


def columns_kernel(meta_ref, count_ref, held_ref, spread_ref, top_out_ref, even_ref, odd_ref):
    @pl.when(leads())
    def _():
        for ref in (even_ref, odd_ref):
            ref[...] = jnp.zeros_like(ref)
        for t in range(held_ref.shape[0]):
            c = meta_ref[1, t]
            scaled = jnp.abs(held_ref[t].astype(jnp.float32)) * spread_ref[row_of(meta_ref, count_ref, t)]
            peak = jnp.max(scaled.reshape(EDGE // 8, 8, EDGE), axis=0)
            ref = (even_ref, odd_ref)[t % 2]
            ref[c] = jnp.maximum(ref[c], peak)
        top_out_ref[...] = jnp.max(jnp.maximum(even_ref[...], odd_ref[...]), axis=1)


def turn_kernel(tiles_ref, turned_ref):
    @pl.when(leads())
    def _():
        for t in range(tiles_ref.shape[0]):
            turned_ref[t] = tiles_ref[t].T


def start_kernel(
    meta_ref, count_ref, tiles_ref, rscale_ref, top_ref, mine_ref, other_ref,
    send_ref, both_ref,
    left_ref, sums_ref, sums_two_ref,
):
    blocks = sums_ref.shape[0]
    sums_refs = (sums_ref, sums_two_ref)
    nrow = ROWBLK * EDGE
    ncol = COLBLK * EDGE

    @pl.when(leads())
    def _():
        both = jnp.concatenate([mine_ref[...], other_ref[...]], axis=0)
        both_ref[...] = both
        clear_left(left_ref)
        adjoint_start(sums_refs, both[:, nrow + ncol :], lax.axis_index("band"))
        for r in range(ROWBLK):
            put_left(left_ref, r, both[:, r * EDGE : (r + 1) * EDGE] * rscale_ref[r : r + 1, :])
        send_ref[0:blocks, :] = top_ref[...]
        for j in range(COLBLK):
            at = (1 + VECS) * blocks + j * VECS
            send_ref[at : at + VECS, :] = both[:, nrow + j * EDGE : nrow + (j + 1) * EDGE]
        tile_pass(meta_ref, count_ref, tiles_ref, left_ref, True, sums_refs)
        for v in range(VECS):
            send_ref[(1 + v) * blocks : (2 + v) * blocks, :] = adjoint_sum(sums_refs, v)


def combined(refs, blocks):
    peak = functools.reduce(jnp.maximum, [ref[0:blocks, :] for ref in refs])
    rows = slice(blocks, (1 + VECS) * blocks)
    return peak, functools.reduce(jnp.add, [ref[rows, :] for ref in refs])


def merge_kernel(blocks, *refs):
    refs, out_ref = refs[:-1], refs[-1]
    head = (1 + VECS) * blocks
    peak, total = combined(refs, blocks)
    out_ref[0:blocks, :] = peak
    out_ref[blocks:head, :] = total
    more = refs[0].shape[0] - head
    for i, ref in enumerate(refs):
        out_ref[head + i * more : head + (i + 1) * more, :] = ref[head:, :]


def step_kernel(
    offsets, parts, meta_ref, count_ref, tiles_ref, turned_ref, *rest,
):
    got_refs = rest[:parts]
    (
        rscale_ref, both_ref, bound_ref,
        send_ref, x_one_ref, cscale_ref, y_one_ref, moved_ref,
        start_ref, right32_ref, right_ref, out_ref, out_two_ref, left_ref, sums_ref, sums_two_ref,
    ) = rest[parts:]
    blocks = right32_ref.shape[0]
    head = (1 + VECS) * blocks
    sums_refs = (sums_ref, sums_two_ref)

    @pl.when(leads())
    def _():
        band = lax.axis_index("band")
        clear_left(left_ref)
        adjoint_start(sums_refs, both_ref[:, (ROWBLK + COLBLK) * EDGE :], band)
        per = len(offsets) // parts
        for m, offset in enumerate(offsets):
            for j in range(COLBLK):
                at = head + (m % per) * COLBLK * VECS + j * VECS
                place = (band ^ offset) * COLBLK + j
                start_ref[place, 0:VECS, :] = got_refs[m // per][at : at + VECS, :]
        start = start_ref.reshape(blocks * 8, EDGE)

        peak, totals = combined(got_refs, blocks)
        cscale = lax.rsqrt(peak)
        cscale_ref[...] = cscale
        for v in range(VECS):
            before = start[pl.ds(v, blocks, stride=8), :]
            after = jnp.maximum(
                0.0, before + step_size * (cscale * totals[v * blocks : (v + 1) * blocks])
            )
            x_one_ref[v * blocks : (v + 1) * blocks, :] = after
            moved = jnp.sum(
                jnp.sum((after - before) ** 2, axis=0, keepdims=True), axis=1, keepdims=True
            )
            moved_ref[v : v + 1, :] = jnp.broadcast_to(moved, (1, EDGE))
            forward_left(right32_ref, v, cscale * (2.0 * after - before))
        for c in range(blocks):
            pair_blocks(right_ref, c, right32_ref[c])

        for ref in (out_ref, out_two_ref):
            ref[...] = jnp.zeros_like(ref)
        tile_pass(meta_ref, count_ref, turned_ref, right_ref, False, (out_ref, out_two_ref))

        moved = jnp.zeros((VECS, EDGE), jnp.float32)
        for r in range(ROWBLK):
            span = slice(r * EDGE, (r + 1) * EDGE)
            scale = rscale_ref[r : r + 1, :]
            before = both_ref[:, span]
            after = jnp.maximum(
                0.0, before + step_size * (scale * (bound_ref[:, span] - joined(out_ref[r] + out_two_ref[r])))
            )
            y_one_ref[:, span] = after
            moved += (after - before) ** 2
            put_left(left_ref, r, after * scale)

        tile_pass(meta_ref, count_ref, tiles_ref, left_ref, True, sums_refs)
        for v in range(VECS):
            send_ref[v * blocks : (v + 1) * blocks, :] = adjoint_sum(sums_refs, v)
        send_ref[VECS * blocks :, :] = jnp.zeros((8, EDGE), jnp.float32)
        send_ref[VECS * blocks : VECS * blocks + VECS, :] = moved


def last_kernel(parts, meta_ref, count_ref, turned_ref, *rest):
    got_refs = rest[:parts]
    (
        rscale_ref, y_ref, bound_ref, x_one_ref, cscale_ref, moved_ref,
        mine_ref, other_ref,
        right32_ref, right_ref, out_ref, out_two_ref,
    ) = rest[parts:]
    blocks = right32_ref.shape[0]
    half = VECS // 2
    ncol = COLBLK * EDGE

    @pl.when(leads())
    def _():
        band = lax.axis_index("band")
        cscale = cscale_ref[...]
        row = lax.broadcasted_iota(jnp.int32, (blocks, EDGE), 0)
        got = functools.reduce(jnp.add, [ref[...] for ref in got_refs])
        dual = jnp.sum(got[VECS * blocks : VECS * blocks + VECS], axis=1, keepdims=True)
        ratio = jnp.sqrt((dual + 1e-06) / (moved_ref[...] + 1e-06))
        for v in range(VECS):
            before = x_one_ref[v * blocks : (v + 1) * blocks, :]
            after = jnp.maximum(
                0.0,
                before
                + step_size / ratio[v : v + 1, :] * (cscale * got[v * blocks : (v + 1) * blocks]),
            )
            to_ref = mine_ref if v < half else other_ref
            for j in range(COLBLK):
                own = jnp.where(row == band * COLBLK + j, after, 0.0)
                to_ref[v % half : v % half + 1, j * EDGE : (j + 1) * EDGE] = jnp.sum(
                    own, axis=0, keepdims=True
                )
            forward_left(right32_ref, v, cscale * (2.0 * after - before))
        for c in range(blocks):
            pair_blocks(right_ref, c, right32_ref[c])

        for ref in (out_ref, out_two_ref):
            ref[...] = jnp.zeros_like(ref)
        tile_pass(meta_ref, count_ref, turned_ref, right_ref, False, (out_ref, out_two_ref))

        for r in range(ROWBLK):
            span = slice(r * EDGE, (r + 1) * EDGE)
            scale = rscale_ref[r : r + 1, :]
            after = jnp.maximum(
                0.0,
                y_ref[:, span]
                + step_size * ratio * (scale * (bound_ref[:, span] - joined(out_ref[r] + out_two_ref[r]))),
            )
            place = slice(ncol + r * EDGE, ncol + (r + 1) * EDGE)
            mine_ref[:, place] = after[0:half]
            other_ref[:, place] = after[half:]


def finish_kernel(mine_ref, got_ref, x_ref, y_ref, sems):
    ncol = x_ref.shape[1]

    def give(from_ref):
        copies = [
            pltpu.make_async_copy(from_ref.at[:, 0:ncol], x_ref, sems.at[0]),
            pltpu.make_async_copy(from_ref.at[:, ncol:], y_ref, sems.at[1]),
        ]
        for copy in copies:
            copy.start()
        for copy in copies:
            copy.wait()

    pl.when(leads())(lambda: give(mine_ref))
    pl.when(jnp.logical_not(leads()))(lambda: give(got_ref))


def swap(value):
    count = lax.axis_size("batch")
    return lax.ppermute(value, "batch", [(i, i ^ 1) for i in range(count)])


def from_band(value, hop):
    bands, batches = lax.axis_size("band"), lax.axis_size("batch")
    pairs = []
    for band in range(bands):
        for batch in range(batches):
            if batch % 2 == 1:
                to = (band ^ hop) * batches + batch
            else:
                to = band * batches + (batch + 2) % batches if batches % 4 == 0 else (band ^ hop) * batches + batch
            pairs.append((band * batches + batch, to))
    return lax.ppermute(value, ("band", "batch"), pairs)


def rounds_of(bands):
    rounds, bit = [], 1
    while bit < bands:
        if bit * 2 < bands:
            rounds.append((bit, 2 * bit, 3 * bit))
        else:
            rounds.append((bit,))
        bit *= 4
    return rounds


def shards(tiles, tile_row, tile_col, tile_count, cost, bound_vec, x_start, y_start):
    tiles = tiles[0]
    ntile = tiles.shape[0]
    bands = lax.axis_size("band")
    blocks = bands * COLBLK
    bound = bound_vec.reshape(1, -1)
    nrow = bound.shape[1]
    f32 = lambda *shape: jax.ShapeDtypeStruct(shape, jnp.float32)
    v32 = lambda *shape: pltpu.VMEM(shape, jnp.float32)
    v16 = lambda *shape: pltpu.VMEM(shape, jnp.bfloat16)
    smem = [pl.BlockSpec(memory_space=pltpu.SMEM)]
    hbm = lambda n: [pl.BlockSpec(memory_space=pltpu.HBM)] * n
    vmem = lambda n: [pl.BlockSpec(memory_space=pltpu.VMEM)] * n
    left = [v16(2 * (ROWBLK + 1), 2 * KEPT, EDGE)]
    right = [v32(blocks, KEPT, EDGE), v16(2 * blocks, 2 * KEPT, EDGE)]
    rows_out = [v32(ROWBLK + 1, KEPT, EDGE)] * 2
    sums = [v32(blocks, KEPT, EDGE)] * 2
    params = pltpu.CompilerParams(vmem_limit_bytes=32 * 1024 * 1024)
    in_hbm = lambda value: pltpu.with_memory_space_constraint(value, pltpu.HBM)

    tile_cost = pl.CostEstimate(flops=0, bytes_accessed=tiles.nbytes, transcendentals=0)
    meta, mine, held, spread, rscale = pl.pallas_call(
        scale_kernel,
        out_shape=(
            pltpu.SMEM((2, ntile), jnp.int32),
            v32(VECS // 2, nrow + 2 * COLBLK * EDGE),
            v16(*tiles.shape),
            v32(ROWBLK + 1, EDGE, EDGE),
            v32(ROWBLK, EDGE),
        ),
        in_specs=hbm(2) + smem + hbm(4),
        out_specs=tuple(smem + vmem(4)),
        scratch_shapes=[
            pltpu.SemaphoreType.DMA((5,)),
            pltpu.SemaphoreType.DMA((ntile // FETCH,)),
            v16(ROWBLK + 1, EDGE, EDGE),
            v16(ROWBLK + 1, EDGE, EDGE),
        ],
        compiler_params=params,
        cost_estimate=tile_cost,
        name="row_scales",
    )(in_hbm(tile_row), in_hbm(tile_col), tile_count, *map(in_hbm, (y_start, x_start, cost, tiles)))
    other = swap(mine)

    top = pl.pallas_call(
        columns_kernel,
        out_shape=v32(blocks, EDGE),
        in_specs=smem * 2 + vmem(2),
        out_specs=vmem(1)[0],
        scratch_shapes=[v32(blocks, 8, EDGE)] * 2,
        compiler_params=params,
        cost_estimate=tile_cost,
        name="columns",
    )(meta, tile_count, held, spread)

    turned = pl.pallas_call(
        turn_kernel,
        out_shape=v16(*tiles.shape),
        in_specs=vmem(1),
        out_specs=vmem(1)[0],
        compiler_params=params,
        cost_estimate=tile_cost,
        name="turn",
    )(held)

    message, both = pl.pallas_call(
        start_kernel,
        out_shape=(f32((1 + VECS) * blocks + COLBLK * VECS, EDGE), v32(VECS, mine.shape[1])),
        in_specs=smem * 2 + vmem(5),
        out_specs=tuple(vmem(2)),
        scratch_shapes=left + sums,
        compiler_params=params,
        name="start",
    )(meta, tile_count, held, rscale, top, mine, other)

    rounds = rounds_of(bands)
    offsets = [0]
    for index, hops in enumerate(rounds):
        messages = [message] + [from_band(message, hop) for hop in hops]
        offsets = [hop ^ offset for hop in (0, *hops) for offset in offsets]
        if index < len(rounds) - 1:
            message = pl.pallas_call(
                functools.partial(merge_kernel, blocks),
                out_shape=f32((1 + VECS) * blocks + COLBLK * VECS * len(offsets), EDGE),
                in_specs=vmem(len(messages)),
                out_specs=vmem(1)[0],
                compiler_params=params,
                name="merge",
            )(*messages)

    message, x_one, cscale, y_one, moved = pl.pallas_call(
        functools.partial(step_kernel, offsets, len(messages)),
        out_shape=(
            f32(VECS * blocks + 8, EDGE), v32(VECS * blocks, EDGE), v32(blocks, EDGE), v32(VECS, nrow), v32(VECS, EDGE),
        ),
        in_specs=smem * 2 + vmem(5 + len(messages)),
        out_specs=tuple(vmem(5)),
        scratch_shapes=[v32(blocks, 8, EDGE)] + right + rows_out + left + sums,
        compiler_params=params,
        name="first_step",
    )(meta, tile_count, held, turned, *messages, rscale, both, bound)

    for index, hops in enumerate(rounds):
        messages = [message] + [from_band(message, hop) for hop in hops]
        if index < len(rounds) - 1:
            message = functools.reduce(jnp.add, messages)

    half = VECS // 2
    width = COLBLK * EDGE + nrow
    mine, other = pl.pallas_call(
        functools.partial(last_kernel, len(messages)),
        out_shape=(v32(half, width), v32(half, width)),
        in_specs=smem * 2 + vmem(7 + len(messages)),
        out_specs=tuple(vmem(2)),
        scratch_shapes=right + rows_out,
        compiler_params=params,
        name="second_step",
    )(meta, tile_count, turned, *messages, rscale, y_one, bound, x_one, cscale, moved)

    return pl.pallas_call(
        finish_kernel,
        out_shape=(f32(*x_start.shape), f32(*y_start.shape)),
        in_specs=vmem(2),
        out_specs=tuple(hbm(2)),
        scratch_shapes=[pltpu.SemaphoreType.DMA((2,))],
        compiler_params=params,
        name="finish",
    )(mine, pltpu.with_memory_space_constraint(swap(other), pltpu.VMEM))


def solution(mesh):
    return jax.shard_map(
        shards,
        mesh=mesh,
        in_specs=(
            P("band", None, None, None),
            P("band", None),
            P("band", None),
            P("band"),
            P("batch", "band"),
            P("band"),
            P("batch", "band"),
            P("batch", "band"),
        ),
        out_specs=(P("batch", "band"), P("batch", "band")),
        check_vma=False,
    )
```

```python
import functools

import jax
import jax.numpy as jnp
from jax import lax
from jax.experimental import pallas as pl
from jax.experimental.pallas import tpu as pltpu
from jax.sharding import PartitionSpec as P

ROWBLK = 4
COLBLK = 2
EDGE = 128
VECS = 4
TERMS = 2
KEPT = VECS * TERMS
FETCH = 8

step_size = 0.0625


def split(value):
    high = value.astype(jnp.bfloat16).astype(jnp.float32)
    return high, (value - high).astype(jnp.bfloat16).astype(jnp.float32)


def joined(rows):
    return rows[0:VECS] + rows[VECS : 2 * VECS]


def leads():
    return lax.axis_index("batch") % 2 == 1


def pair_blocks(ref, index, rows):
    count = ref.shape[0] // 2
    empty = jnp.zeros_like(rows)
    ref[index] = jnp.concatenate([rows, empty], axis=0).astype(jnp.bfloat16)
    ref[count + index] = jnp.concatenate([empty, rows], axis=0).astype(jnp.bfloat16)


def put_left(left_ref, index, value):
    pair_blocks(left_ref, index, jnp.concatenate(split(value), axis=0))


def clear_left(left_ref):
    pair_blocks(left_ref, ROWBLK, jnp.zeros((KEPT, EDGE), jnp.float32))


def adjoint_start(sums_refs, costs, band):
    for ref in sums_refs:
        ref[...] = jnp.zeros_like(ref)
    for j in range(COLBLK):
        sums_refs[0][band * COLBLK + j, 0:VECS, :] = -costs[:, j * EDGE : (j + 1) * EDGE]


def adjoint_sum(sums_refs, v):
    blocks = sums_refs[0].shape[0]
    total = 0.0
    for ref in sums_refs:
        flat = ref.reshape(blocks * KEPT, EDGE)
        for s in range(TERMS):
            total += flat[pl.ds(VECS * s + v, blocks, stride=KEPT), :]
    return total


def forward_left(right32_ref, v, value):
    blocks = right32_ref.shape[0]
    flat = right32_ref.reshape(blocks * KEPT, EDGE)
    for s, term in enumerate(split(value)):
        flat[pl.ds(VECS * s + v, blocks, stride=KEPT), :] = term


def row_of(meta_ref, count_ref, t):
    return jnp.where(t < count_ref[0], meta_ref[0, t], ROWBLK)


def tile_pass(meta_ref, count_ref, tiles_ref, left_ref, of_row, into_refs):
    count = left_ref.shape[0] // 2
    for t in range(0, tiles_ref.shape[0], 2):
        rows = [row_of(meta_ref, count_ref, t + u) for u in range(2)]
        cols = [meta_ref[1, t + u] for u in range(2)]
        source, place = (rows, cols) if of_row else (cols, rows)
        left = jnp.concatenate([left_ref[source[0]], left_ref[count + source[1]]], axis=1)
        pair = tiles_ref[t : t + 2].reshape(2 * EDGE, EDGE)
        product = jnp.dot(left, pair, preferred_element_type=jnp.float32)
        for u in range(2):
            part = product[u * KEPT : (u + 1) * KEPT]
            into_refs[u][place[u]] += jnp.where(rows[u] < ROWBLK, part, 0.0)


def scale_kernel(
    rows_ref, cols_ref, count_ref, y_ref, x_ref, cost_ref, tiles_ref,
    meta_ref, own_ref, held_ref, spread_ref, rscale_ref,
    small_sems, sems, even_ref, odd_ref,
):
    nrow, ncol = y_ref.shape[1], x_ref.shape[1]
    parts = sems.shape[0]
    per = held_ref.shape[0] // parts
    places = [
        pltpu.make_async_copy(rows_ref, meta_ref.at[0:1], small_sems.at[0]),
        pltpu.make_async_copy(cols_ref, meta_ref.at[1:2], small_sems.at[1]),
    ]
    vectors = [
        pltpu.make_async_copy(y_ref, own_ref.at[:, 0:nrow], small_sems.at[2]),
        pltpu.make_async_copy(x_ref, own_ref.at[:, nrow : nrow + ncol], small_sems.at[3]),
        pltpu.make_async_copy(cost_ref, own_ref.at[:, nrow + ncol :], small_sems.at[4]),
    ]
    for copy in places:
        copy.start()

    @pl.when(leads())
    def _():
        peak_refs = (even_ref, odd_ref)
        fetches = []
        for g in range(parts):
            part = pl.ds(g * per, per)
            fetches.append(pltpu.make_async_copy(tiles_ref.at[part], held_ref.at[part], sems.at[g]))
            fetches[g].start()
        for copy in vectors:
            copy.start()
        for ref in peak_refs:
            ref[...] = jnp.zeros_like(ref)
        spread_ref[ROWBLK] = jnp.zeros((EDGE, EDGE), jnp.float32)
        for copy in places:
            copy.wait()
        for t in range(held_ref.shape[0]):
            if t % per == 0:
                fetches[t // per].wait()
            r = row_of(meta_ref, count_ref, t)
            tile = held_ref[t]
            ref = peak_refs[t % 2]
            ref[r] = jnp.maximum(ref[r], jnp.maximum(tile, -tile))
        for r in range(ROWBLK):
            peak = jnp.maximum(even_ref[r], odd_ref[r])
            turned = jnp.max(peak.T.astype(jnp.float32), axis=0, keepdims=True)
            rscale_ref[r : r + 1, :] = lax.rsqrt(turned)
            peak = jnp.max(peak.astype(jnp.float32), axis=1, keepdims=True)
            spread_ref[r] = lax.rsqrt(jnp.broadcast_to(peak, (EDGE, EDGE)))
        for copy in vectors:
            copy.wait()

    @pl.when(jnp.logical_not(leads()))
    def _():
        for copy in vectors:
            copy.start()
        for copy in places + vectors:
            copy.wait()


def columns_kernel(meta_ref, count_ref, held_ref, spread_ref, top_out_ref, even_ref, odd_ref):
    @pl.when(leads())
    def _():
        for ref in (even_ref, odd_ref):
            ref[...] = jnp.zeros_like(ref)
        for t in range(held_ref.shape[0]):
            c = meta_ref[1, t]
            scaled = jnp.abs(held_ref[t].astype(jnp.float32)) * spread_ref[row_of(meta_ref, count_ref, t)]
            peak = jnp.max(scaled.reshape(EDGE // 8, 8, EDGE), axis=0)
            ref = (even_ref, odd_ref)[t % 2]
            ref[c] = jnp.maximum(ref[c], peak)
        top_out_ref[...] = jnp.max(jnp.maximum(even_ref[...], odd_ref[...]), axis=1)


def turn_kernel(tiles_ref, turned_ref):
    @pl.when(leads())
    def _():
        for t in range(tiles_ref.shape[0]):
            turned_ref[t] = tiles_ref[t].T


def start_kernel(
    meta_ref, count_ref, tiles_ref, rscale_ref, top_ref, mine_ref, other_ref,
    send_ref, both_ref,
    left_ref, sums_ref, sums_two_ref,
):
    blocks = sums_ref.shape[0]
    sums_refs = (sums_ref, sums_two_ref)
    nrow = ROWBLK * EDGE
    ncol = COLBLK * EDGE

    @pl.when(leads())
    def _():
        both = jnp.concatenate([mine_ref[...], other_ref[...]], axis=0)
        both_ref[...] = both
        clear_left(left_ref)
        adjoint_start(sums_refs, both[:, nrow + ncol :], lax.axis_index("band"))
        for r in range(ROWBLK):
            put_left(left_ref, r, both[:, r * EDGE : (r + 1) * EDGE] * rscale_ref[r : r + 1, :])
        send_ref[0:blocks, :] = top_ref[...]
        for j in range(COLBLK):
            at = (1 + VECS) * blocks + j * VECS
            send_ref[at : at + VECS, :] = both[:, nrow + j * EDGE : nrow + (j + 1) * EDGE]
        tile_pass(meta_ref, count_ref, tiles_ref, left_ref, True, sums_refs)
        for v in range(VECS):
            send_ref[(1 + v) * blocks : (2 + v) * blocks, :] = adjoint_sum(sums_refs, v)


def combined(refs, blocks):
    peak = functools.reduce(jnp.maximum, [ref[0:blocks, :] for ref in refs])
    rows = slice(blocks, (1 + VECS) * blocks)
    return peak, functools.reduce(jnp.add, [ref[rows, :] for ref in refs])


def merge_kernel(blocks, turned_ref, *refs):
    refs, out_ref = refs[:-1], refs[-1]
    head = (1 + VECS) * blocks
    peak, total = combined(refs, blocks)
    out_ref[0:blocks, :] = peak
    out_ref[blocks:head, :] = total
    more = refs[0].shape[0] - head
    for i, ref in enumerate(refs):
        out_ref[head + i * more : head + (i + 1) * more, :] = ref[head:, :]


def step_kernel(
    offsets, parts, meta_ref, count_ref, tiles_ref, turned_ref, *rest,
):
    got_refs = rest[:parts]
    (
        rscale_ref, both_ref, bound_ref,
        send_ref, x_one_ref, cscale_ref, y_one_ref, moved_ref,
        start_ref, right32_ref, right_ref, out_ref, out_two_ref, left_ref, sums_ref, sums_two_ref,
    ) = rest[parts:]
    blocks = right32_ref.shape[0]
    head = (1 + VECS) * blocks
    sums_refs = (sums_ref, sums_two_ref)

    @pl.when(leads())
    def _():
        band = lax.axis_index("band")
        clear_left(left_ref)
        adjoint_start(sums_refs, both_ref[:, (ROWBLK + COLBLK) * EDGE :], band)
        per = len(offsets) // parts
        for m, offset in enumerate(offsets):
            for j in range(COLBLK):
                at = head + (m % per) * COLBLK * VECS + j * VECS
                place = (band ^ offset) * COLBLK + j
                start_ref[place, 0:VECS, :] = got_refs[m // per][at : at + VECS, :]
        start = start_ref.reshape(blocks * 8, EDGE)

        peak, totals = combined(got_refs, blocks)
        cscale = lax.rsqrt(peak)
        cscale_ref[...] = cscale
        for v in range(VECS):
            before = start[pl.ds(v, blocks, stride=8), :]
            after = jnp.maximum(
                0.0, before + step_size * (cscale * totals[v * blocks : (v + 1) * blocks])
            )
            x_one_ref[v * blocks : (v + 1) * blocks, :] = after
            moved = jnp.sum(
                jnp.sum((after - before) ** 2, axis=0, keepdims=True), axis=1, keepdims=True
            )
            moved_ref[v : v + 1, :] = jnp.broadcast_to(moved, (1, EDGE))
            forward_left(right32_ref, v, cscale * (2.0 * after - before))
        for c in range(blocks):
            pair_blocks(right_ref, c, right32_ref[c])

        for ref in (out_ref, out_two_ref):
            ref[...] = jnp.zeros_like(ref)
        tile_pass(meta_ref, count_ref, turned_ref, right_ref, False, (out_ref, out_two_ref))

        moved = jnp.zeros((VECS, EDGE), jnp.float32)
        for r in range(ROWBLK):
            span = slice(r * EDGE, (r + 1) * EDGE)
            scale = rscale_ref[r : r + 1, :]
            before = both_ref[:, span]
            after = jnp.maximum(
                0.0, before + step_size * (scale * (bound_ref[:, span] - joined(out_ref[r] + out_two_ref[r])))
            )
            y_one_ref[:, span] = after
            moved += (after - before) ** 2
            put_left(left_ref, r, after * scale)

        tile_pass(meta_ref, count_ref, tiles_ref, left_ref, True, sums_refs)
        for v in range(VECS):
            send_ref[v * blocks : (v + 1) * blocks, :] = adjoint_sum(sums_refs, v)
        send_ref[VECS * blocks :, :] = jnp.zeros((8, EDGE), jnp.float32)
        send_ref[VECS * blocks : VECS * blocks + VECS, :] = moved


def last_kernel(parts, meta_ref, count_ref, turned_ref, *rest):
    got_refs = rest[:parts]
    (
        rscale_ref, y_ref, bound_ref, x_one_ref, cscale_ref, moved_ref,
        mine_ref, other_ref,
        right32_ref, right_ref, out_ref, out_two_ref,
    ) = rest[parts:]
    blocks = right32_ref.shape[0]
    half = VECS // 2
    ncol = COLBLK * EDGE

    @pl.when(leads())
    def _():
        band = lax.axis_index("band")
        cscale = cscale_ref[...]
        row = lax.broadcasted_iota(jnp.int32, (blocks, EDGE), 0)
        got = functools.reduce(jnp.add, [ref[...] for ref in got_refs])
        dual = jnp.sum(got[VECS * blocks : VECS * blocks + VECS], axis=1, keepdims=True)
        ratio = jnp.sqrt((dual + 1e-06) / (moved_ref[...] + 1e-06))
        for v in range(VECS):
            before = x_one_ref[v * blocks : (v + 1) * blocks, :]
            after = jnp.maximum(
                0.0,
                before
                + step_size / ratio[v : v + 1, :] * (cscale * got[v * blocks : (v + 1) * blocks]),
            )
            to_ref = mine_ref if v < half else other_ref
            for j in range(COLBLK):
                own = jnp.where(row == band * COLBLK + j, after, 0.0)
                to_ref[v % half : v % half + 1, j * EDGE : (j + 1) * EDGE] = jnp.sum(
                    own, axis=0, keepdims=True
                )
            forward_left(right32_ref, v, cscale * (2.0 * after - before))
        for c in range(blocks):
            pair_blocks(right_ref, c, right32_ref[c])

        for ref in (out_ref, out_two_ref):
            ref[...] = jnp.zeros_like(ref)
        tile_pass(meta_ref, count_ref, turned_ref, right_ref, False, (out_ref, out_two_ref))

        for r in range(ROWBLK):
            span = slice(r * EDGE, (r + 1) * EDGE)
            scale = rscale_ref[r : r + 1, :]
            after = jnp.maximum(
                0.0,
                y_ref[:, span]
                + step_size * ratio * (scale * (bound_ref[:, span] - joined(out_ref[r] + out_two_ref[r]))),
            )
            place = slice(ncol + r * EDGE, ncol + (r + 1) * EDGE)
            mine_ref[:, place] = after[0:half]
            other_ref[:, place] = after[half:]


def finish_kernel(mine_ref, got_ref, x_ref, y_ref, sems):
    ncol = x_ref.shape[1]

    def give(from_ref):
        copies = [
            pltpu.make_async_copy(from_ref.at[:, 0:ncol], x_ref, sems.at[0]),
            pltpu.make_async_copy(from_ref.at[:, ncol:], y_ref, sems.at[1]),
        ]
        for copy in copies:
            copy.start()
        for copy in copies:
            copy.wait()

    pl.when(leads())(lambda: give(mine_ref))
    pl.when(jnp.logical_not(leads()))(lambda: give(got_ref))


def swap(value):
    count = lax.axis_size("batch")
    return lax.ppermute(value, "batch", [(i, i ^ 1) for i in range(count)])


def from_band(value, hop):
    bands, batches = lax.axis_size("band"), lax.axis_size("batch")
    pairs = []
    for band in range(bands):
        for batch in range(batches):
            if batch % 2 == 1:
                to = (band ^ hop) * batches + batch
            else:
                to = band * batches + (batch + 2) % batches if batches % 4 == 0 else (band ^ hop) * batches + batch
            pairs.append((band * batches + batch, to))
    return lax.ppermute(value, ("band", "batch"), pairs)


def rounds_of(bands):
    rounds, bit = [], 1
    while bit < bands:
        if bit * 2 < bands:
            rounds.append((bit, 2 * bit, 3 * bit))
        else:
            rounds.append((bit,))
        bit *= 4
    return rounds[::-1]


def shards(tiles, tile_row, tile_col, tile_count, cost, bound_vec, x_start, y_start):
    tiles = tiles[0]
    ntile = tiles.shape[0]
    bands = lax.axis_size("band")
    blocks = bands * COLBLK
    bound = bound_vec.reshape(1, -1)
    nrow = bound.shape[1]
    f32 = lambda *shape: jax.ShapeDtypeStruct(shape, jnp.float32)
    v32 = lambda *shape: pltpu.VMEM(shape, jnp.float32)
    v16 = lambda *shape: pltpu.VMEM(shape, jnp.bfloat16)
    smem = [pl.BlockSpec(memory_space=pltpu.SMEM)]
    hbm = lambda n: [pl.BlockSpec(memory_space=pltpu.HBM)] * n
    vmem = lambda n: [pl.BlockSpec(memory_space=pltpu.VMEM)] * n
    left = [v16(2 * (ROWBLK + 1), 2 * KEPT, EDGE)]
    right = [v32(blocks, KEPT, EDGE), v16(2 * blocks, 2 * KEPT, EDGE)]
    rows_out = [v32(ROWBLK + 1, KEPT, EDGE)] * 2
    sums = [v32(blocks, KEPT, EDGE)] * 2
    params = pltpu.CompilerParams(vmem_limit_bytes=32 * 1024 * 1024)
    in_hbm = lambda value: pltpu.with_memory_space_constraint(value, pltpu.HBM)

    tile_cost = pl.CostEstimate(flops=0, bytes_accessed=tiles.nbytes, transcendentals=0)
    meta, mine, held, spread, rscale = pl.pallas_call(
        scale_kernel,
        out_shape=(
            pltpu.SMEM((2, ntile), jnp.int32),
            v32(VECS // 2, nrow + 2 * COLBLK * EDGE),
            v16(*tiles.shape),
            v32(ROWBLK + 1, EDGE, EDGE),
            v32(ROWBLK, EDGE),
        ),
        in_specs=hbm(2) + smem + hbm(4),
        out_specs=tuple(smem + vmem(4)),
        scratch_shapes=[
            pltpu.SemaphoreType.DMA((5,)),
            pltpu.SemaphoreType.DMA((ntile // FETCH,)),
            v16(ROWBLK + 1, EDGE, EDGE),
            v16(ROWBLK + 1, EDGE, EDGE),
        ],
        compiler_params=params,
        cost_estimate=tile_cost,
        name="row_scales",
    )(in_hbm(tile_row), in_hbm(tile_col), tile_count, *map(in_hbm, (y_start, x_start, cost, tiles)))
    other = swap(mine)

    top = pl.pallas_call(
        columns_kernel,
        out_shape=v32(blocks, EDGE),
        in_specs=smem * 2 + vmem(2),
        out_specs=vmem(1)[0],
        scratch_shapes=[v32(blocks, 8, EDGE)] * 2,
        compiler_params=params,
        cost_estimate=tile_cost,
        name="columns",
    )(meta, tile_count, held, spread)

    turned = pl.pallas_call(
        turn_kernel,
        out_shape=v16(*tiles.shape),
        in_specs=vmem(1),
        out_specs=vmem(1)[0],
        compiler_params=params,
        cost_estimate=tile_cost,
        name="turn",
    )(held)

    message, both = pl.pallas_call(
        start_kernel,
        out_shape=(f32((1 + VECS) * blocks + COLBLK * VECS, EDGE), v32(VECS, mine.shape[1])),
        in_specs=smem * 2 + vmem(5),
        out_specs=tuple(vmem(2)),
        scratch_shapes=left + sums,
        compiler_params=params,
        name="start",
    )(meta, tile_count, held, rscale, top, mine, other)

    rounds = rounds_of(bands)
    offsets = [0]
    for index, hops in enumerate(rounds):
        messages = [message] + [from_band(message, hop) for hop in hops]
        offsets = [hop ^ offset for hop in (0, *hops) for offset in offsets]
        if index < len(rounds) - 1:
            message = pl.pallas_call(
                functools.partial(merge_kernel, blocks),
                out_shape=f32((1 + VECS) * blocks + COLBLK * VECS * len(offsets), EDGE),
                in_specs=vmem(1 + len(messages)),
                out_specs=vmem(1)[0],
                compiler_params=params,
                name="merge",
            )(turned, *messages)

    message, x_one, cscale, y_one, moved = pl.pallas_call(
        functools.partial(step_kernel, offsets, len(messages)),
        out_shape=(
            f32(VECS * blocks + 8, EDGE), v32(VECS * blocks, EDGE), v32(blocks, EDGE), v32(VECS, nrow), v32(VECS, EDGE),
        ),
        in_specs=smem * 2 + vmem(5 + len(messages)),
        out_specs=tuple(vmem(5)),
        scratch_shapes=[v32(blocks, 8, EDGE)] + right + rows_out + left + sums,
        compiler_params=params,
        name="first_step",
    )(meta, tile_count, held, turned, *messages, rscale, both, bound)

    for index, hops in enumerate(rounds):
        messages = [message] + [from_band(message, hop) for hop in hops]
        if index < len(rounds) - 1:
            message = functools.reduce(jnp.add, messages)

    half = VECS // 2
    width = COLBLK * EDGE + nrow
    mine, other = pl.pallas_call(
        functools.partial(last_kernel, len(messages)),
        out_shape=(v32(half, width), v32(half, width)),
        in_specs=smem * 2 + vmem(7 + len(messages)),
        out_specs=tuple(vmem(2)),
        scratch_shapes=right + rows_out,
        compiler_params=params,
        name="second_step",
    )(meta, tile_count, turned, *messages, rscale, y_one, bound, x_one, cscale, moved)

    return pl.pallas_call(
        finish_kernel,
        out_shape=(f32(*x_start.shape), f32(*y_start.shape)),
        in_specs=vmem(2),
        out_specs=tuple(hbm(2)),
        scratch_shapes=[pltpu.SemaphoreType.DMA((2,))],
        compiler_params=params,
        name="finish",
    )(mine, pltpu.with_memory_space_constraint(swap(other), pltpu.VMEM))


def solution(mesh):
    return jax.shard_map(
        shards,
        mesh=mesh,
        in_specs=(
            P("band", None, None, None),
            P("band", None),
            P("band", None),
            P("band"),
            P("batch", "band"),
            P("band"),
            P("batch", "band"),
            P("batch", "band"),
        ),
        out_specs=(P("batch", "band"), P("batch", "band")),
        check_vma=False,
    )
```

```python
import functools

import jax
import jax.numpy as jnp
from jax import lax
from jax.experimental import pallas as pl
from jax.experimental.pallas import tpu as pltpu
from jax.sharding import PartitionSpec as P

ROWBLK = 4
COLBLK = 2
EDGE = 128
VECS = 4
TERMS = 2
KEPT = VECS * TERMS
FETCH = 8

step_size = 0.0625


def split(value):
    high = value.astype(jnp.bfloat16).astype(jnp.float32)
    return high, (value - high).astype(jnp.bfloat16).astype(jnp.float32)


def joined(rows):
    return rows[0:VECS] + rows[VECS : 2 * VECS]


def leads():
    return lax.axis_index("batch") % 2 == 1


def pair_blocks(ref, index, rows):
    count = ref.shape[0] // 2
    empty = jnp.zeros_like(rows)
    ref[index] = jnp.concatenate([rows, empty], axis=0).astype(jnp.bfloat16)
    ref[count + index] = jnp.concatenate([empty, rows], axis=0).astype(jnp.bfloat16)


def put_left(left_ref, index, value):
    pair_blocks(left_ref, index, jnp.concatenate(split(value), axis=0))


def clear_left(left_ref):
    pair_blocks(left_ref, ROWBLK, jnp.zeros((KEPT, EDGE), jnp.float32))


def adjoint_start(sums_refs, costs, band):
    for ref in sums_refs:
        ref[...] = jnp.zeros_like(ref)
    for j in range(COLBLK):
        sums_refs[0][band * COLBLK + j, 0:VECS, :] = -costs[:, j * EDGE : (j + 1) * EDGE]


def adjoint_sum(sums_refs, v):
    blocks = sums_refs[0].shape[0]
    total = 0.0
    for ref in sums_refs:
        flat = ref.reshape(blocks * KEPT, EDGE)
        for s in range(TERMS):
            total += flat[pl.ds(VECS * s + v, blocks, stride=KEPT), :]
    return total


def forward_left(right32_ref, v, value):
    blocks = right32_ref.shape[0]
    flat = right32_ref.reshape(blocks * KEPT, EDGE)
    for s, term in enumerate(split(value)):
        flat[pl.ds(VECS * s + v, blocks, stride=KEPT), :] = term


def row_of(meta_ref, count_ref, t):
    return jnp.where(t < count_ref[0], meta_ref[0, t], ROWBLK)


def tile_pass(meta_ref, count_ref, tiles_ref, left_ref, of_row, into_refs):
    count = left_ref.shape[0] // 2
    for t in range(0, tiles_ref.shape[0], 2):
        rows = [row_of(meta_ref, count_ref, t + u) for u in range(2)]
        cols = [meta_ref[1, t + u] for u in range(2)]
        source, place = (rows, cols) if of_row else (cols, rows)
        left = jnp.concatenate([left_ref[source[0]], left_ref[count + source[1]]], axis=1)
        pair = tiles_ref[t : t + 2].reshape(2 * EDGE, EDGE)
        product = jnp.dot(left, pair, preferred_element_type=jnp.float32)
        for u in range(2):
            part = product[u * KEPT : (u + 1) * KEPT]
            into_refs[u][place[u]] += jnp.where(rows[u] < ROWBLK, part, 0.0)


def scale_kernel(
    rows_ref, cols_ref, count_ref, y_ref, x_ref, cost_ref, tiles_ref,
    meta_ref, own_ref, held_ref, spread_ref, rscale_ref,
    small_sems, sems, even_ref, odd_ref,
):
    nrow, ncol = y_ref.shape[1], x_ref.shape[1]
    parts = sems.shape[0]
    per = held_ref.shape[0] // parts
    places = [
        pltpu.make_async_copy(rows_ref, meta_ref.at[0:1], small_sems.at[0]),
        pltpu.make_async_copy(cols_ref, meta_ref.at[1:2], small_sems.at[1]),
    ]
    vectors = [
        pltpu.make_async_copy(y_ref, own_ref.at[:, 0:nrow], small_sems.at[2]),
        pltpu.make_async_copy(x_ref, own_ref.at[:, nrow : nrow + ncol], small_sems.at[3]),
        pltpu.make_async_copy(cost_ref, own_ref.at[:, nrow + ncol :], small_sems.at[4]),
    ]
    for copy in places:
        copy.start()

    @pl.when(leads())
    def _():
        peak_refs = (even_ref, odd_ref)
        fetches = []
        for g in range(parts):
            part = pl.ds(g * per, per)
            fetches.append(pltpu.make_async_copy(tiles_ref.at[part], held_ref.at[part], sems.at[g]))
            fetches[g].start()
        for copy in vectors:
            copy.start()
        for ref in peak_refs:
            ref[...] = jnp.zeros_like(ref)
        spread_ref[ROWBLK] = jnp.zeros((EDGE, EDGE), jnp.float32)
        for copy in places:
            copy.wait()
        for t in range(held_ref.shape[0]):
            if t % per == 0:
                fetches[t // per].wait()
            r = row_of(meta_ref, count_ref, t)
            tile = held_ref[t]
            ref = peak_refs[t % 2]
            ref[r] = jnp.maximum(ref[r], jnp.maximum(tile, -tile))
        for r in range(ROWBLK):
            peak = jnp.maximum(even_ref[r], odd_ref[r])
            turned = jnp.max(peak.T.astype(jnp.float32), axis=0, keepdims=True)
            rscale_ref[r : r + 1, :] = lax.rsqrt(turned)
            peak = jnp.max(peak.astype(jnp.float32), axis=1, keepdims=True)
            spread_ref[r] = lax.rsqrt(jnp.broadcast_to(peak, (EDGE, EDGE)))
        for copy in vectors:
            copy.wait()

    @pl.when(jnp.logical_not(leads()))
    def _():
        for copy in vectors:
            copy.start()
        for copy in places + vectors:
            copy.wait()


def columns_kernel(meta_ref, count_ref, held_ref, spread_ref, top_out_ref, even_ref, odd_ref):
    @pl.when(leads())
    def _():
        for ref in (even_ref, odd_ref):
            ref[...] = jnp.zeros_like(ref)
        for t in range(held_ref.shape[0]):
            c = meta_ref[1, t]
            scaled = jnp.abs(held_ref[t].astype(jnp.float32)) * spread_ref[row_of(meta_ref, count_ref, t)]
            peak = jnp.max(scaled.reshape(EDGE // 8, 8, EDGE), axis=0)
            ref = (even_ref, odd_ref)[t % 2]
            ref[c] = jnp.maximum(ref[c], peak)
        top_out_ref[...] = jnp.max(jnp.maximum(even_ref[...], odd_ref[...]), axis=1)


def turn_kernel(tiles_ref, turned_ref):
    @pl.when(leads())
    def _():
        for t in range(tiles_ref.shape[0]):
            turned_ref[t] = tiles_ref[t].T


def start_kernel(
    meta_ref, count_ref, tiles_ref, rscale_ref, top_ref, mine_ref, other_ref,
    send_ref, both_ref,
    left_ref, sums_ref, sums_two_ref,
):
    blocks = sums_ref.shape[0]
    sums_refs = (sums_ref, sums_two_ref)
    nrow = ROWBLK * EDGE
    ncol = COLBLK * EDGE

    @pl.when(leads())
    def _():
        both = jnp.concatenate([mine_ref[...], other_ref[...]], axis=0)
        both_ref[...] = both
        clear_left(left_ref)
        adjoint_start(sums_refs, both[:, nrow + ncol :], lax.axis_index("band"))
        for r in range(ROWBLK):
            put_left(left_ref, r, both[:, r * EDGE : (r + 1) * EDGE] * rscale_ref[r : r + 1, :])
        send_ref[0:blocks, :] = top_ref[...]
        for j in range(COLBLK):
            at = (1 + VECS) * blocks + j * VECS
            send_ref[at : at + VECS, :] = both[:, nrow + j * EDGE : nrow + (j + 1) * EDGE]
        tile_pass(meta_ref, count_ref, tiles_ref, left_ref, True, sums_refs)
        for v in range(VECS):
            send_ref[(1 + v) * blocks : (2 + v) * blocks, :] = adjoint_sum(sums_refs, v)


def combined(refs, blocks):
    peak = functools.reduce(jnp.maximum, [ref[0:blocks, :] for ref in refs])
    rows = slice(blocks, (1 + VECS) * blocks)
    return peak, functools.reduce(jnp.add, [ref[rows, :] for ref in refs])


def merge_kernel(blocks, *refs):
    refs, out_ref = refs[:-1], refs[-1]
    head = (1 + VECS) * blocks
    peak, total = combined(refs, blocks)
    out_ref[0:blocks, :] = peak
    out_ref[blocks:head, :] = total
    more = refs[0].shape[0] - head
    for i, ref in enumerate(refs):
        out_ref[head + i * more : head + (i + 1) * more, :] = ref[head:, :]


def step_kernel(
    offsets, parts, meta_ref, count_ref, tiles_ref, turned_ref, *rest,
):
    got_refs = rest[:parts]
    (
        rscale_ref, both_ref, bound_ref,
        send_ref, x_one_ref, cscale_ref, y_one_ref, moved_ref,
        start_ref, right32_ref, right_ref, out_ref, out_two_ref, left_ref, sums_ref, sums_two_ref,
    ) = rest[parts:]
    blocks = right32_ref.shape[0]
    head = (1 + VECS) * blocks
    sums_refs = (sums_ref, sums_two_ref)

    @pl.when(leads())
    def _():
        band = lax.axis_index("band")
        clear_left(left_ref)
        adjoint_start(sums_refs, both_ref[:, (ROWBLK + COLBLK) * EDGE :], band)
        per = len(offsets) // parts
        for m, offset in enumerate(offsets):
            for j in range(COLBLK):
                at = head + (m % per) * COLBLK * VECS + j * VECS
                place = (band ^ offset) * COLBLK + j
                start_ref[place, 0:VECS, :] = got_refs[m // per][at : at + VECS, :]
        start = start_ref.reshape(blocks * 8, EDGE)

        peak, totals = combined(got_refs, blocks)
        cscale = lax.rsqrt(peak)
        cscale_ref[...] = cscale
        for v in range(VECS):
            before = start[pl.ds(v, blocks, stride=8), :]
            after = jnp.maximum(
                0.0, before + step_size * (cscale * totals[v * blocks : (v + 1) * blocks])
            )
            x_one_ref[v * blocks : (v + 1) * blocks, :] = after
            moved = jnp.sum(
                jnp.sum((after - before) ** 2, axis=0, keepdims=True), axis=1, keepdims=True
            )
            moved_ref[v : v + 1, :] = jnp.broadcast_to(moved, (1, EDGE))
            forward_left(right32_ref, v, cscale * (2.0 * after - before))
        for c in range(blocks):
            pair_blocks(right_ref, c, right32_ref[c])

        for ref in (out_ref, out_two_ref):
            ref[...] = jnp.zeros_like(ref)
        tile_pass(meta_ref, count_ref, turned_ref, right_ref, False, (out_ref, out_two_ref))

        moved = jnp.zeros((VECS, EDGE), jnp.float32)
        for r in range(ROWBLK):
            span = slice(r * EDGE, (r + 1) * EDGE)
            scale = rscale_ref[r : r + 1, :]
            before = both_ref[:, span]
            after = jnp.maximum(
                0.0, before + step_size * (scale * (bound_ref[:, span] - joined(out_ref[r] + out_two_ref[r])))
            )
            y_one_ref[:, span] = after
            moved += (after - before) ** 2
            put_left(left_ref, r, after * scale)

        tile_pass(meta_ref, count_ref, tiles_ref, left_ref, True, sums_refs)
        for v in range(VECS):
            send_ref[v * blocks : (v + 1) * blocks, :] = adjoint_sum(sums_refs, v)
        send_ref[VECS * blocks :, :] = jnp.zeros((8, EDGE), jnp.float32)
        send_ref[VECS * blocks : VECS * blocks + VECS, :] = moved


def last_kernel(parts, meta_ref, count_ref, turned_ref, *rest):
    got_refs = rest[:parts]
    (
        rscale_ref, y_ref, bound_ref, x_one_ref, cscale_ref, moved_ref,
        mine_ref, other_ref,
        right32_ref, right_ref, out_ref, out_two_ref,
    ) = rest[parts:]
    blocks = right32_ref.shape[0]
    half = VECS // 2
    ncol = COLBLK * EDGE

    @pl.when(leads())
    def _():
        band = lax.axis_index("band")
        cscale = cscale_ref[...]
        row = lax.broadcasted_iota(jnp.int32, (blocks, EDGE), 0)
        got = functools.reduce(jnp.add, [ref[...] for ref in got_refs])
        dual = jnp.sum(got[VECS * blocks : VECS * blocks + VECS], axis=1, keepdims=True)
        ratio = jnp.sqrt((dual + 1e-06) / (moved_ref[...] + 1e-06))
        for v in range(VECS):
            before = x_one_ref[v * blocks : (v + 1) * blocks, :]
            after = jnp.maximum(
                0.0,
                before
                + step_size / ratio[v : v + 1, :] * (cscale * got[v * blocks : (v + 1) * blocks]),
            )
            to_ref = mine_ref if v < half else other_ref
            for j in range(COLBLK):
                own = jnp.where(row == band * COLBLK + j, after, 0.0)
                to_ref[v % half : v % half + 1, j * EDGE : (j + 1) * EDGE] = jnp.sum(
                    own, axis=0, keepdims=True
                )
            forward_left(right32_ref, v, cscale * (2.0 * after - before))
        for c in range(blocks):
            pair_blocks(right_ref, c, right32_ref[c])

        for ref in (out_ref, out_two_ref):
            ref[...] = jnp.zeros_like(ref)
        tile_pass(meta_ref, count_ref, turned_ref, right_ref, False, (out_ref, out_two_ref))

        for r in range(ROWBLK):
            span = slice(r * EDGE, (r + 1) * EDGE)
            scale = rscale_ref[r : r + 1, :]
            after = jnp.maximum(
                0.0,
                y_ref[:, span]
                + step_size * ratio * (scale * (bound_ref[:, span] - joined(out_ref[r] + out_two_ref[r]))),
            )
            place = slice(ncol + r * EDGE, ncol + (r + 1) * EDGE)
            mine_ref[:, place] = after[0:half]
            other_ref[:, place] = after[half:]


def finish_kernel(mine_ref, got_ref, x_ref, y_ref, sems):
    ncol = x_ref.shape[1]

    def give(from_ref):
        copies = [
            pltpu.make_async_copy(from_ref.at[:, 0:ncol], x_ref, sems.at[0]),
            pltpu.make_async_copy(from_ref.at[:, ncol:], y_ref, sems.at[1]),
        ]
        for copy in copies:
            copy.start()
        for copy in copies:
            copy.wait()

    pl.when(leads())(lambda: give(mine_ref))
    pl.when(jnp.logical_not(leads()))(lambda: give(got_ref))


def swap(value):
    count = lax.axis_size("batch")
    return lax.ppermute(value, "batch", [(i, i ^ 1) for i in range(count)])


def relayed(value, hop, side):
    bands, batches = lax.axis_size("band"), lax.axis_size("batch")
    pairs = []
    for band in range(bands):
        for batch in range(batches):
            to = band ^ hop if batch % 2 == side else band
            pairs.append((band * batches + batch, to * batches + (batch ^ 1)))
    return lax.ppermute(value, ("band", "batch"), pairs)


def gathered(value, hops, side):
    return [swap(value)] + [relayed(value, hop, side) for hop in hops]


def rounds_of(bands):
    rounds, bit = [], 1
    while bit < bands:
        if bit * 2 < bands:
            rounds.append((bit, 2 * bit, 3 * bit))
        else:
            rounds.append((bit,))
        bit *= 4
    return rounds if len(rounds) % 2 == 0 else rounds + [()]


def shards(tiles, tile_row, tile_col, tile_count, cost, bound_vec, x_start, y_start):
    tiles = tiles[0]
    ntile = tiles.shape[0]
    bands = lax.axis_size("band")
    blocks = bands * COLBLK
    bound = bound_vec.reshape(1, -1)
    nrow = bound.shape[1]
    f32 = lambda *shape: jax.ShapeDtypeStruct(shape, jnp.float32)
    v32 = lambda *shape: pltpu.VMEM(shape, jnp.float32)
    v16 = lambda *shape: pltpu.VMEM(shape, jnp.bfloat16)
    smem = [pl.BlockSpec(memory_space=pltpu.SMEM)]
    hbm = lambda n: [pl.BlockSpec(memory_space=pltpu.HBM)] * n
    vmem = lambda n: [pl.BlockSpec(memory_space=pltpu.VMEM)] * n
    left = [v16(2 * (ROWBLK + 1), 2 * KEPT, EDGE)]
    right = [v32(blocks, KEPT, EDGE), v16(2 * blocks, 2 * KEPT, EDGE)]
    rows_out = [v32(ROWBLK + 1, KEPT, EDGE)] * 2
    sums = [v32(blocks, KEPT, EDGE)] * 2
    params = pltpu.CompilerParams(vmem_limit_bytes=32 * 1024 * 1024)
    in_hbm = lambda value: pltpu.with_memory_space_constraint(value, pltpu.HBM)

    tile_cost = pl.CostEstimate(flops=0, bytes_accessed=tiles.nbytes, transcendentals=0)
    meta, mine, held, spread, rscale = pl.pallas_call(
        scale_kernel,
        out_shape=(
            pltpu.SMEM((2, ntile), jnp.int32),
            v32(VECS // 2, nrow + 2 * COLBLK * EDGE),
            v16(*tiles.shape),
            v32(ROWBLK + 1, EDGE, EDGE),
            v32(ROWBLK, EDGE),
        ),
        in_specs=hbm(2) + smem + hbm(4),
        out_specs=tuple(smem + vmem(4)),
        scratch_shapes=[
            pltpu.SemaphoreType.DMA((5,)),
            pltpu.SemaphoreType.DMA((ntile // FETCH,)),
            v16(ROWBLK + 1, EDGE, EDGE),
            v16(ROWBLK + 1, EDGE, EDGE),
        ],
        compiler_params=params,
        cost_estimate=tile_cost,
        name="row_scales",
    )(in_hbm(tile_row), in_hbm(tile_col), tile_count, *map(in_hbm, (y_start, x_start, cost, tiles)))
    other = swap(mine)

    top = pl.pallas_call(
        columns_kernel,
        out_shape=v32(blocks, EDGE),
        in_specs=smem * 2 + vmem(2),
        out_specs=vmem(1)[0],
        scratch_shapes=[v32(blocks, 8, EDGE)] * 2,
        compiler_params=params,
        cost_estimate=tile_cost,
        name="columns",
    )(meta, tile_count, held, spread)

    turned = pl.pallas_call(
        turn_kernel,
        out_shape=v16(*tiles.shape),
        in_specs=vmem(1),
        out_specs=vmem(1)[0],
        compiler_params=params,
        cost_estimate=tile_cost,
        name="turn",
    )(held)

    message, both = pl.pallas_call(
        start_kernel,
        out_shape=(f32((1 + VECS) * blocks + COLBLK * VECS, EDGE), v32(VECS, mine.shape[1])),
        in_specs=smem * 2 + vmem(5),
        out_specs=tuple(vmem(2)),
        scratch_shapes=left + sums,
        compiler_params=params,
        name="start",
    )(meta, tile_count, held, rscale, top, mine, other)

    rounds = rounds_of(bands)
    offsets = [0]
    for index, hops in enumerate(rounds):
        messages = gathered(message, hops, (index + 1) % 2)
        offsets = [hop ^ offset for hop in (0, *hops) for offset in offsets]
        if index < len(rounds) - 1:
            message = pl.pallas_call(
                functools.partial(merge_kernel, blocks),
                out_shape=f32((1 + VECS) * blocks + COLBLK * VECS * len(offsets), EDGE),
                in_specs=vmem(len(messages)),
                out_specs=vmem(1)[0],
                compiler_params=params,
                name="merge",
            )(*messages)

    message, x_one, cscale, y_one, moved = pl.pallas_call(
        functools.partial(step_kernel, offsets, len(messages)),
        out_shape=(
            f32(VECS * blocks + 8, EDGE), v32(VECS * blocks, EDGE), v32(blocks, EDGE), v32(VECS, nrow), v32(VECS, EDGE),
        ),
        in_specs=smem * 2 + vmem(5 + len(messages)),
        out_specs=tuple(vmem(5)),
        scratch_shapes=[v32(blocks, 8, EDGE)] + right + rows_out + left + sums,
        compiler_params=params,
        name="first_step",
    )(meta, tile_count, held, turned, *messages, rscale, both, bound)

    for index, hops in enumerate(rounds):
        messages = gathered(message, hops, (index + 1) % 2)
        if index < len(rounds) - 1:
            message = functools.reduce(jnp.add, messages)

    half = VECS // 2
    width = COLBLK * EDGE + nrow
    mine, other = pl.pallas_call(
        functools.partial(last_kernel, len(messages)),
        out_shape=(v32(half, width), v32(half, width)),
        in_specs=smem * 2 + vmem(7 + len(messages)),
        out_specs=tuple(vmem(2)),
        scratch_shapes=right + rows_out,
        compiler_params=params,
        name="second_step",
    )(meta, tile_count, turned, *messages, rscale, y_one, bound, x_one, cscale, moved)

    return pl.pallas_call(
        finish_kernel,
        out_shape=(f32(*x_start.shape), f32(*y_start.shape)),
        in_specs=vmem(2),
        out_specs=tuple(hbm(2)),
        scratch_shapes=[pltpu.SemaphoreType.DMA((2,))],
        compiler_params=params,
        name="finish",
    )(mine, pltpu.with_memory_space_constraint(swap(other), pltpu.VMEM))


def solution(mesh):
    return jax.shard_map(
        shards,
        mesh=mesh,
        in_specs=(
            P("band", None, None, None),
            P("band", None),
            P("band", None),
            P("band"),
            P("batch", "band"),
            P("band"),
            P("batch", "band"),
            P("batch", "band"),
        ),
        out_specs=(P("batch", "band"), P("batch", "band")),
        check_vma=False,
    )
```

```python
import functools

import jax
import jax.numpy as jnp
from jax import lax
from jax.experimental import pallas as pl
from jax.experimental.pallas import tpu as pltpu
from jax.sharding import PartitionSpec as P

ROWBLK = 4
COLBLK = 2
EDGE = 128
VECS = 4
TERMS = 2
KEPT = VECS * TERMS
FETCH = 8

step_size = 0.0625


def split(value):
    high = value.astype(jnp.bfloat16).astype(jnp.float32)
    return high, (value - high).astype(jnp.bfloat16).astype(jnp.float32)


def joined(rows):
    return rows[0:VECS] + rows[VECS : 2 * VECS]


def leads():
    return lax.axis_index("batch") % 2 == 1


def pair_blocks(ref, index, rows):
    count = ref.shape[0] // 2
    empty = jnp.zeros_like(rows)
    ref[index] = jnp.concatenate([rows, empty], axis=0).astype(jnp.bfloat16)
    ref[count + index] = jnp.concatenate([empty, rows], axis=0).astype(jnp.bfloat16)


def clear_left(left_ref):
    pair_blocks(left_ref, ROWBLK, jnp.zeros((KEPT, EDGE), jnp.float32))


def adjoint_start(sums_refs, costs, band):
    for ref in sums_refs:
        ref[...] = jnp.zeros_like(ref)
    for j in range(COLBLK):
        sums_refs[0][band * COLBLK + j, 0:VECS, :] = -costs[:, j * EDGE : (j + 1) * EDGE]


def adjoint_sum(sums_refs, c):
    return sum(joined(ref[c]) for ref in sums_refs)


def span(c):
    return slice(c * EDGE, (c + 1) * EDGE)


def put_block(ref, index, value):
    pair_blocks(ref, index, jnp.concatenate(split(value), axis=0))


def row_of(meta_ref, count_ref, t):
    return jnp.where(t < count_ref[0], meta_ref[0, t], ROWBLK)


def tile_pass(meta_ref, count_ref, tiles_ref, left_ref, of_row, into_refs):
    count = left_ref.shape[0] // 2
    for t in range(0, tiles_ref.shape[0], 2):
        rows = [row_of(meta_ref, count_ref, t + u) for u in range(2)]
        cols = [meta_ref[1, t + u] for u in range(2)]
        source, place = (rows, cols) if of_row else (cols, rows)
        left = jnp.concatenate([left_ref[source[0]], left_ref[count + source[1]]], axis=1)
        pair = tiles_ref[t : t + 2].reshape(2 * EDGE, EDGE)
        product = jnp.dot(left, pair, preferred_element_type=jnp.float32)
        for u in range(2):
            part = product[u * KEPT : (u + 1) * KEPT]
            into_refs[u][place[u]] += jnp.where(rows[u] < ROWBLK, part, 0.0)


def scale_kernel(
    rows_ref, cols_ref, count_ref, y_ref, x_ref, cost_ref, tiles_ref,
    meta_ref, own_ref, held_ref, spread_ref, rscale_ref,
    small_sems, sems, even_ref, odd_ref,
):
    nrow, ncol = y_ref.shape[1], x_ref.shape[1]
    parts = sems.shape[0]
    per = held_ref.shape[0] // parts
    places = [
        pltpu.make_async_copy(rows_ref, meta_ref.at[0:1], small_sems.at[0]),
        pltpu.make_async_copy(cols_ref, meta_ref.at[1:2], small_sems.at[1]),
    ]
    vectors = [
        pltpu.make_async_copy(y_ref, own_ref.at[:, 0:nrow], small_sems.at[2]),
        pltpu.make_async_copy(x_ref, own_ref.at[:, nrow : nrow + ncol], small_sems.at[3]),
        pltpu.make_async_copy(cost_ref, own_ref.at[:, nrow + ncol :], small_sems.at[4]),
    ]
    for copy in places:
        copy.start()

    @pl.when(leads())
    def _():
        peak_refs = (even_ref, odd_ref)
        fetches = []
        for g in range(parts):
            part = pl.ds(g * per, per)
            fetches.append(pltpu.make_async_copy(tiles_ref.at[part], held_ref.at[part], sems.at[g]))
            fetches[g].start()
        for copy in vectors:
            copy.start()
        for ref in peak_refs:
            ref[...] = jnp.zeros_like(ref)
        spread_ref[ROWBLK] = jnp.zeros((EDGE, EDGE), jnp.float32)
        for copy in places:
            copy.wait()
        for t in range(held_ref.shape[0]):
            if t % per == 0:
                fetches[t // per].wait()
            r = row_of(meta_ref, count_ref, t)
            tile = held_ref[t]
            ref = peak_refs[t % 2]
            ref[r] = jnp.maximum(ref[r], jnp.maximum(tile, -tile))
        for r in range(ROWBLK):
            peak = jnp.maximum(even_ref[r], odd_ref[r])
            turned = jnp.max(peak.T.astype(jnp.float32), axis=0, keepdims=True)
            rscale_ref[r : r + 1, :] = lax.rsqrt(turned)
            peak = jnp.max(peak.astype(jnp.float32), axis=1, keepdims=True)
            spread_ref[r] = lax.rsqrt(jnp.broadcast_to(peak, (EDGE, EDGE)))
        for copy in vectors:
            copy.wait()

    @pl.when(jnp.logical_not(leads()))
    def _():
        for copy in vectors:
            copy.start()
        for copy in places + vectors:
            copy.wait()


def columns_kernel(meta_ref, count_ref, held_ref, spread_ref, top_out_ref, even_ref, odd_ref):
    @pl.when(leads())
    def _():
        for ref in (even_ref, odd_ref):
            ref[...] = jnp.zeros_like(ref)
        for t in range(held_ref.shape[0]):
            c = meta_ref[1, t]
            scaled = jnp.abs(held_ref[t].astype(jnp.float32)) * spread_ref[row_of(meta_ref, count_ref, t)]
            peak = jnp.max(scaled.reshape(EDGE // 8, 8, EDGE), axis=0)
            ref = (even_ref, odd_ref)[t % 2]
            ref[c] = jnp.maximum(ref[c], peak)
        top_out_ref[...] = jnp.max(jnp.maximum(even_ref[...], odd_ref[...]), axis=1)


def turn_kernel(tiles_ref, turned_ref):
    @pl.when(leads())
    def _():
        for t in range(tiles_ref.shape[0]):
            turned_ref[t] = tiles_ref[t].T


def start_kernel(
    meta_ref, count_ref, tiles_ref, rscale_ref, top_ref, mine_ref, other_ref,
    send_ref, both_ref,
    left_ref, sums_ref, sums_two_ref,
):
    blocks = sums_ref.shape[0]
    sums_refs = (sums_ref, sums_two_ref)
    nrow = ROWBLK * EDGE
    ncol = COLBLK * EDGE

    @pl.when(leads())
    def _():
        both = jnp.concatenate([mine_ref[...], other_ref[...]], axis=0)
        both_ref[...] = both
        clear_left(left_ref)
        adjoint_start(sums_refs, both[:, nrow + ncol :], lax.axis_index("band"))
        for r in range(ROWBLK):
            put_block(left_ref, r, both[:, r * EDGE : (r + 1) * EDGE] * rscale_ref[r : r + 1, :])
        per = blocks // VECS
        for m in range(per):
            send_ref[:, span(blocks + m)] = top_ref[pl.ds(m, VECS, stride=per), :]
        send_ref[:, (blocks + per) * EDGE :] = both[:, nrow : nrow + ncol]
        tile_pass(meta_ref, count_ref, tiles_ref, left_ref, True, sums_refs)
        for c in range(blocks):
            send_ref[:, span(c)] = adjoint_sum(sums_refs, c)


def peaks_of(refs, blocks):
    spot = slice(blocks * EDGE, (blocks + blocks // VECS) * EDGE)
    return functools.reduce(jnp.maximum, [ref[:, spot] for ref in refs])


def merge_kernel(blocks, *refs):
    refs, out_ref = refs[:-1], refs[-1]
    head = (blocks + blocks // VECS) * EDGE
    out_ref[:, blocks * EDGE : head] = peaks_of(refs, blocks)
    for c in range(blocks):
        out_ref[:, span(c)] = functools.reduce(jnp.add, [ref[:, span(c)] for ref in refs])
    more = refs[0].shape[1] - head
    for i, ref in enumerate(refs):
        out_ref[:, head + i * more : head + (i + 1) * more] = ref[:, head:]


def step_kernel(
    offsets, parts, meta_ref, count_ref, tiles_ref, turned_ref, *rest,
):
    got_refs = rest[:parts]
    (
        rscale_ref, both_ref, bound_ref,
        send_ref, x_one_ref, cscale_ref, y_one_ref, moved_ref,
        start_ref, right_ref, out_ref, out_two_ref, left_ref, sums_ref, sums_two_ref,
    ) = rest[parts:]
    blocks = start_ref.shape[0]
    places = blocks // VECS
    head = (blocks + places) * EDGE
    sums_refs = (sums_ref, sums_two_ref)

    @pl.when(leads())
    def _():
        band = lax.axis_index("band")
        clear_left(left_ref)
        adjoint_start(sums_refs, both_ref[:, (ROWBLK + COLBLK) * EDGE :], band)
        per = len(offsets) // parts
        for m, offset in enumerate(offsets):
            for j in range(COLBLK):
                at = head + ((m % per) * COLBLK + j) * EDGE
                start_ref[(band ^ offset) * COLBLK + j] = got_refs[m // per][:, at : at + EDGE]

        cscale = lax.rsqrt(peaks_of(got_refs, blocks))
        cscale_ref[...] = cscale
        moved = jnp.zeros((VECS, EDGE), jnp.float32)
        for c in range(blocks):
            scale = cscale[c // places : c // places + 1, span(c % places)]
            total = functools.reduce(jnp.add, [ref[:, span(c)] for ref in got_refs])
            before = start_ref[c]
            after = jnp.maximum(0.0, before + step_size * (scale * total))
            x_one_ref[:, span(c)] = after
            moved += (after - before) ** 2
            put_block(right_ref, c, scale * (2.0 * after - before))
        moved_ref[...] = moved

        for ref in (out_ref, out_two_ref):
            ref[...] = jnp.zeros_like(ref)
        tile_pass(meta_ref, count_ref, turned_ref, right_ref, False, (out_ref, out_two_ref))

        moved = jnp.zeros((VECS, EDGE), jnp.float32)
        for r in range(ROWBLK):
            scale = rscale_ref[r : r + 1, :]
            before = both_ref[:, span(r)]
            after = jnp.maximum(
                0.0, before + step_size * (scale * (bound_ref[:, span(r)] - joined(out_ref[r] + out_two_ref[r])))
            )
            y_one_ref[:, span(r)] = after
            moved += (after - before) ** 2
            put_block(left_ref, r, after * scale)

        tile_pass(meta_ref, count_ref, tiles_ref, left_ref, True, sums_refs)
        for c in range(blocks):
            send_ref[:, span(c)] = adjoint_sum(sums_refs, c)
        send_ref[:, blocks * EDGE :] = moved


def last_kernel(parts, meta_ref, count_ref, turned_ref, *rest):
    got_refs = rest[:parts]
    (
        rscale_ref, y_ref, bound_ref, x_one_ref, cscale_ref, moved_ref,
        mine_ref, other_ref,
        own_ref, right_ref, out_ref, out_two_ref,
    ) = rest[parts:]
    blocks = own_ref.shape[0]
    places = blocks // VECS
    half = VECS // 2
    ncol = COLBLK * EDGE

    @pl.when(leads())
    def _():
        band = lax.axis_index("band")
        dual = functools.reduce(jnp.add, [ref[:, blocks * EDGE :] for ref in got_refs])
        dual = jnp.sum(dual, axis=1, keepdims=True)
        primal = jnp.sum(moved_ref[...], axis=1, keepdims=True)
        ratio = jnp.sqrt((dual + 1e-06) / (primal + 1e-06))
        size = step_size / ratio
        for c in range(blocks):
            scale = cscale_ref[c // places : c // places + 1, span(c % places)]
            total = functools.reduce(jnp.add, [ref[:, span(c)] for ref in got_refs])
            before = x_one_ref[:, span(c)]
            after = jnp.maximum(0.0, before + size * (scale * total))
            own_ref[c] = after
            put_block(right_ref, c, scale * (2.0 * after - before))
        for j in range(COLBLK):
            own = own_ref[band * COLBLK + j]
            mine_ref[:, span(j)] = own[0:half]
            other_ref[:, span(j)] = own[half:]

        for ref in (out_ref, out_two_ref):
            ref[...] = jnp.zeros_like(ref)
        tile_pass(meta_ref, count_ref, turned_ref, right_ref, False, (out_ref, out_two_ref))

        for r in range(ROWBLK):
            scale = rscale_ref[r : r + 1, :]
            after = jnp.maximum(
                0.0,
                y_ref[:, span(r)]
                + step_size * ratio * (scale * (bound_ref[:, span(r)] - joined(out_ref[r] + out_two_ref[r]))),
            )
            place = slice(ncol + r * EDGE, ncol + (r + 1) * EDGE)
            mine_ref[:, place] = after[0:half]
            other_ref[:, place] = after[half:]


def finish_kernel(mine_ref, got_ref, x_ref, y_ref, sems):
    ncol = x_ref.shape[1]

    def give(from_ref):
        copies = [
            pltpu.make_async_copy(from_ref.at[:, 0:ncol], x_ref, sems.at[0]),
            pltpu.make_async_copy(from_ref.at[:, ncol:], y_ref, sems.at[1]),
        ]
        for copy in copies:
            copy.start()
        for copy in copies:
            copy.wait()

    pl.when(leads())(lambda: give(mine_ref))
    pl.when(jnp.logical_not(leads()))(lambda: give(got_ref))


def swap(value):
    count = lax.axis_size("batch")
    return lax.ppermute(value, "batch", [(i, i ^ 1) for i in range(count)])


def relayed(value, hop, side):
    bands, batches = lax.axis_size("band"), lax.axis_size("batch")
    pairs = []
    for band in range(bands):
        for batch in range(batches):
            to = band ^ hop if batch % 2 == side else band
            pairs.append((band * batches + batch, to * batches + (batch ^ 1)))
    return lax.ppermute(value, ("band", "batch"), pairs)


def gathered(value, hops, side):
    return [swap(value)] + [relayed(value, hop, side) for hop in hops]


def rounds_of(bands):
    rounds, bit = [], 1
    while bit < bands:
        if bit * 2 < bands:
            rounds.append((bit, 2 * bit, 3 * bit))
        else:
            rounds.append((bit,))
        bit *= 4
    return rounds if len(rounds) % 2 == 0 else rounds + [()]


def shards(tiles, tile_row, tile_col, tile_count, cost, bound_vec, x_start, y_start):
    tiles = tiles[0]
    ntile = tiles.shape[0]
    bands = lax.axis_size("band")
    blocks = bands * COLBLK
    head = (blocks + blocks // VECS) * EDGE
    bound = bound_vec.reshape(1, -1)
    nrow = bound.shape[1]
    f32 = lambda *shape: jax.ShapeDtypeStruct(shape, jnp.float32)
    v32 = lambda *shape: pltpu.VMEM(shape, jnp.float32)
    v16 = lambda *shape: pltpu.VMEM(shape, jnp.bfloat16)
    smem = [pl.BlockSpec(memory_space=pltpu.SMEM)]
    hbm = lambda n: [pl.BlockSpec(memory_space=pltpu.HBM)] * n
    vmem = lambda n: [pl.BlockSpec(memory_space=pltpu.VMEM)] * n
    left = [v16(2 * (ROWBLK + 1), 2 * KEPT, EDGE)]
    right = [v32(blocks, VECS, EDGE), v16(2 * blocks, 2 * KEPT, EDGE)]
    rows_out = [v32(ROWBLK + 1, KEPT, EDGE)] * 2
    sums = [v32(blocks, KEPT, EDGE)] * 2
    params = pltpu.CompilerParams(vmem_limit_bytes=32 * 1024 * 1024)
    in_hbm = lambda value: pltpu.with_memory_space_constraint(value, pltpu.HBM)

    tile_cost = pl.CostEstimate(flops=0, bytes_accessed=tiles.nbytes, transcendentals=0)
    meta, mine, held, spread, rscale = pl.pallas_call(
        scale_kernel,
        out_shape=(
            pltpu.SMEM((2, ntile), jnp.int32),
            v32(VECS // 2, nrow + 2 * COLBLK * EDGE),
            v16(*tiles.shape),
            v32(ROWBLK + 1, EDGE, EDGE),
            v32(ROWBLK, EDGE),
        ),
        in_specs=hbm(2) + smem + hbm(4),
        out_specs=tuple(smem + vmem(4)),
        scratch_shapes=[
            pltpu.SemaphoreType.DMA((5,)),
            pltpu.SemaphoreType.DMA((ntile // FETCH,)),
            v16(ROWBLK + 1, EDGE, EDGE),
            v16(ROWBLK + 1, EDGE, EDGE),
        ],
        compiler_params=params,
        cost_estimate=tile_cost,
        name="row_scales",
    )(in_hbm(tile_row), in_hbm(tile_col), tile_count, *map(in_hbm, (y_start, x_start, cost, tiles)))
    other = swap(mine)

    top = pl.pallas_call(
        columns_kernel,
        out_shape=v32(blocks, EDGE),
        in_specs=smem * 2 + vmem(2),
        out_specs=vmem(1)[0],
        scratch_shapes=[v32(blocks, 8, EDGE)] * 2,
        compiler_params=params,
        cost_estimate=tile_cost,
        name="columns",
    )(meta, tile_count, held, spread)

    turned = pl.pallas_call(
        turn_kernel,
        out_shape=v16(*tiles.shape),
        in_specs=vmem(1),
        out_specs=vmem(1)[0],
        compiler_params=params,
        cost_estimate=tile_cost,
        name="turn",
    )(held)

    message, both = pl.pallas_call(
        start_kernel,
        out_shape=(f32(VECS, head + COLBLK * EDGE), v32(VECS, mine.shape[1])),
        in_specs=smem * 2 + vmem(5),
        out_specs=tuple(vmem(2)),
        scratch_shapes=left + sums,
        compiler_params=params,
        name="start",
    )(meta, tile_count, held, rscale, top, mine, other)

    rounds = rounds_of(bands)
    offsets = [0]
    for index, hops in enumerate(rounds):
        messages = gathered(message, hops, (index + 1) % 2)
        offsets = [hop ^ offset for hop in (0, *hops) for offset in offsets]
        if index < len(rounds) - 1:
            message = pl.pallas_call(
                functools.partial(merge_kernel, blocks),
                out_shape=f32(VECS, head + len(offsets) * COLBLK * EDGE),
                in_specs=vmem(len(messages)),
                out_specs=vmem(1)[0],
                compiler_params=params,
                name="merge",
            )(*messages)

    message, x_one, cscale, y_one, moved = pl.pallas_call(
        functools.partial(step_kernel, offsets, len(messages)),
        out_shape=(
            f32(VECS, (blocks + 1) * EDGE), v32(VECS, blocks * EDGE), v32(VECS, blocks // VECS * EDGE), v32(VECS, nrow), v32(VECS, EDGE),
        ),
        in_specs=smem * 2 + vmem(5 + len(messages)),
        out_specs=tuple(vmem(5)),
        scratch_shapes=right + rows_out + left + sums,
        compiler_params=params,
        name="first_step",
    )(meta, tile_count, held, turned, *messages, rscale, both, bound)

    for index, hops in enumerate(rounds):
        messages = gathered(message, hops, (index + 1) % 2)
        if index < len(rounds) - 1:
            message = functools.reduce(jnp.add, messages)

    half = VECS // 2
    width = COLBLK * EDGE + nrow
    mine, other = pl.pallas_call(
        functools.partial(last_kernel, len(messages)),
        out_shape=(v32(half, width), v32(half, width)),
        in_specs=smem * 2 + vmem(7 + len(messages)),
        out_specs=tuple(vmem(2)),
        scratch_shapes=right + rows_out,
        compiler_params=params,
        name="second_step",
    )(meta, tile_count, turned, *messages, rscale, y_one, bound, x_one, cscale, moved)

    return pl.pallas_call(
        finish_kernel,
        out_shape=(f32(*x_start.shape), f32(*y_start.shape)),
        in_specs=vmem(2),
        out_specs=tuple(hbm(2)),
        scratch_shapes=[pltpu.SemaphoreType.DMA((2,))],
        compiler_params=params,
        name="finish",
    )(mine, pltpu.with_memory_space_constraint(swap(other), pltpu.VMEM))


def solution(mesh):
    return jax.shard_map(
        shards,
        mesh=mesh,
        in_specs=(
            P("band", None, None, None),
            P("band", None),
            P("band", None),
            P("band"),
            P("batch", "band"),
            P("band"),
            P("batch", "band"),
            P("batch", "band"),
        ),
        out_specs=(P("batch", "band"), P("batch", "band")),
        check_vma=False,
    )
```

```python
import functools

import jax
import jax.numpy as jnp
from jax import lax
from jax.experimental import pallas as pl
from jax.experimental.pallas import tpu as pltpu
from jax.sharding import PartitionSpec as P

ROWBLK = 4
COLBLK = 2
EDGE = 128
VECS = 4
TERMS = 2
KEPT = VECS * TERMS
FETCH = 8

step_size = 0.0625


def split(value):
    high = value.astype(jnp.bfloat16).astype(jnp.float32)
    return high, (value - high).astype(jnp.bfloat16).astype(jnp.float32)


def joined(rows):
    return rows[0:VECS] + rows[VECS : 2 * VECS]


def leads():
    return lax.axis_index("batch") % 2 == 1


def pair_blocks(ref, index, rows):
    count = ref.shape[0] // 2
    empty = jnp.zeros_like(rows)
    ref[index] = jnp.concatenate([rows, empty], axis=0).astype(jnp.bfloat16)
    ref[count + index] = jnp.concatenate([empty, rows], axis=0).astype(jnp.bfloat16)


def clear_left(left_ref):
    pair_blocks(left_ref, ROWBLK, jnp.zeros((KEPT, EDGE), jnp.float32))


def adjoint_start(sums_refs, costs, band):
    for ref in sums_refs:
        ref[...] = jnp.zeros_like(ref)
    for j in range(COLBLK):
        sums_refs[0][band * COLBLK + j, 0:VECS, :] = -costs[:, j * EDGE : (j + 1) * EDGE]


def adjoint_sum(sums_refs, c):
    return sum(joined(ref[c]) for ref in sums_refs)


def span(c):
    return slice(c * EDGE, (c + 1) * EDGE)


def put_block(ref, index, value):
    pair_blocks(ref, index, jnp.concatenate(split(value), axis=0))


def row_of(meta_ref, count_ref, t):
    return jnp.where(t < count_ref[0], meta_ref[0, t], ROWBLK)


def tile_pass(meta_ref, count_ref, tiles_ref, left_ref, of_row, into_refs):
    count = left_ref.shape[0] // 2
    for t in range(0, tiles_ref.shape[0], 2):
        rows = [row_of(meta_ref, count_ref, t + u) for u in range(2)]
        cols = [meta_ref[1, t + u] for u in range(2)]
        source, place = (rows, cols) if of_row else (cols, rows)
        left = jnp.concatenate([left_ref[source[0]], left_ref[count + source[1]]], axis=1)
        pair = tiles_ref[t : t + 2].reshape(2 * EDGE, EDGE)
        product = jnp.dot(left, pair, preferred_element_type=jnp.float32)
        for u in range(2):
            part = product[u * KEPT : (u + 1) * KEPT]
            into_refs[u][place[u]] += jnp.where(rows[u] < ROWBLK, part, 0.0)


def scale_kernel(
    rows_ref, cols_ref, count_ref, y_ref, x_ref, cost_ref, tiles_ref,
    meta_ref, own_ref, held_ref, spread_ref, rscale_ref,
    small_sems, sems, even_ref, odd_ref,
):
    nrow, ncol = y_ref.shape[1], x_ref.shape[1]
    parts = sems.shape[0]
    per = held_ref.shape[0] // parts
    places = [
        pltpu.make_async_copy(rows_ref, meta_ref.at[0:1], small_sems.at[0]),
        pltpu.make_async_copy(cols_ref, meta_ref.at[1:2], small_sems.at[1]),
    ]
    vectors = [
        pltpu.make_async_copy(y_ref, own_ref.at[:, 0:nrow], small_sems.at[2]),
        pltpu.make_async_copy(x_ref, own_ref.at[:, nrow : nrow + ncol], small_sems.at[3]),
        pltpu.make_async_copy(cost_ref, own_ref.at[:, nrow + ncol :], small_sems.at[4]),
    ]
    for copy in places:
        copy.start()

    @pl.when(leads())
    def _():
        peak_refs = (even_ref, odd_ref)
        fetches = []
        for g in range(parts):
            part = pl.ds(g * per, per)
            fetches.append(pltpu.make_async_copy(tiles_ref.at[part], held_ref.at[part], sems.at[g]))
            fetches[g].start()
        for copy in vectors:
            copy.start()
        for ref in peak_refs:
            ref[...] = jnp.zeros_like(ref)
        spread_ref[ROWBLK] = jnp.zeros((EDGE, EDGE), jnp.float32)
        for copy in places:
            copy.wait()
        for t in range(held_ref.shape[0]):
            if t % per == 0:
                fetches[t // per].wait()
            r = row_of(meta_ref, count_ref, t)
            tile = held_ref[t]
            ref = peak_refs[t % 2]
            ref[r] = jnp.maximum(ref[r], jnp.maximum(tile, -tile))
        for r in range(ROWBLK):
            peak = jnp.maximum(even_ref[r], odd_ref[r])
            turned = jnp.max(peak.T.astype(jnp.float32), axis=0, keepdims=True)
            rscale_ref[r : r + 1, :] = lax.rsqrt(turned)
            peak = jnp.max(peak.astype(jnp.float32), axis=1, keepdims=True)
            spread_ref[r] = lax.rsqrt(jnp.broadcast_to(peak, (EDGE, EDGE)))
        for copy in vectors:
            copy.wait()

    @pl.when(jnp.logical_not(leads()))
    def _():
        for copy in vectors:
            copy.start()
        for copy in places + vectors:
            copy.wait()


def columns_kernel(meta_ref, count_ref, held_ref, spread_ref, top_out_ref, even_ref, odd_ref):
    @pl.when(leads())
    def _():
        for ref in (even_ref, odd_ref):
            ref[...] = jnp.zeros_like(ref)
        for t in range(held_ref.shape[0]):
            c = meta_ref[1, t]
            scaled = jnp.abs(held_ref[t].astype(jnp.float32)) * spread_ref[row_of(meta_ref, count_ref, t)]
            peak = jnp.max(scaled.reshape(EDGE // 8, 8, EDGE), axis=0)
            ref = (even_ref, odd_ref)[t % 2]
            ref[c] = jnp.maximum(ref[c], peak)
        top_out_ref[...] = jnp.max(jnp.maximum(even_ref[...], odd_ref[...]), axis=1)


def turn_kernel(tiles_ref, turned_ref):
    @pl.when(leads())
    def _():
        for t in range(tiles_ref.shape[0]):
            turned_ref[t] = tiles_ref[t].T


def start_kernel(
    meta_ref, count_ref, tiles_ref, rscale_ref, top_ref, mine_ref, other_ref,
    send_ref, both_ref,
    left_ref, sums_ref, sums_two_ref,
):
    blocks = sums_ref.shape[0]
    sums_refs = (sums_ref, sums_two_ref)
    nrow = ROWBLK * EDGE
    ncol = COLBLK * EDGE

    @pl.when(leads())
    def _():
        both = jnp.concatenate([mine_ref[...], other_ref[...]], axis=0)
        both_ref[...] = both
        clear_left(left_ref)
        adjoint_start(sums_refs, both[:, nrow + ncol :], lax.axis_index("band"))
        for r in range(ROWBLK):
            put_block(left_ref, r, both[:, r * EDGE : (r + 1) * EDGE] * rscale_ref[r : r + 1, :])
        per = blocks // VECS
        for m in range(per):
            send_ref[:, span(blocks + m)] = top_ref[pl.ds(m, VECS, stride=per), :]
        send_ref[:, (blocks + per) * EDGE :] = both[:, nrow : nrow + ncol]
        tile_pass(meta_ref, count_ref, tiles_ref, left_ref, True, sums_refs)
        for c in range(blocks):
            send_ref[:, span(c)] = adjoint_sum(sums_refs, c)


def peaks_of(refs, blocks):
    spot = slice(blocks * EDGE, (blocks + blocks // VECS) * EDGE)
    return functools.reduce(jnp.maximum, [ref[:, spot] for ref in refs])


def merge_kernel(blocks, *refs):
    refs, out_ref = refs[:-1], refs[-1]
    head = (blocks + blocks // VECS) * EDGE
    out_ref[:, blocks * EDGE : head] = peaks_of(refs, blocks)
    for c in range(blocks):
        out_ref[:, span(c)] = functools.reduce(jnp.add, [ref[:, span(c)] for ref in refs])
    more = refs[0].shape[1] - head
    for i, ref in enumerate(refs):
        out_ref[:, head + i * more : head + (i + 1) * more] = ref[:, head:]


def step_kernel(
    offsets, parts, meta_ref, count_ref, tiles_ref, turned_ref, *rest,
):
    got_refs = rest[:parts]
    (
        rscale_ref, both_ref, bound_ref,
        send_ref, x_one_ref, cscale_ref, y_one_ref, moved_ref,
        start_ref, right_ref, out_ref, out_two_ref, left_ref, sums_ref, sums_two_ref,
    ) = rest[parts:]
    blocks = start_ref.shape[0]
    places = blocks // VECS
    head = (blocks + places) * EDGE
    sums_refs = (sums_ref, sums_two_ref)

    @pl.when(leads())
    def _():
        band = lax.axis_index("band")
        clear_left(left_ref)
        adjoint_start(sums_refs, both_ref[:, (ROWBLK + COLBLK) * EDGE :], band)
        per = len(offsets) // parts
        for m, offset in enumerate(offsets):
            for j in range(COLBLK):
                at = head + ((m % per) * COLBLK + j) * EDGE
                start_ref[(band ^ offset) * COLBLK + j] = got_refs[m // per][:, at : at + EDGE]

        cscale = lax.rsqrt(peaks_of(got_refs, blocks))
        cscale_ref[...] = cscale
        moved = jnp.zeros((VECS, EDGE), jnp.float32)
        for c in range(blocks):
            scale = cscale[c // places : c // places + 1, span(c % places)]
            total = functools.reduce(jnp.add, [ref[:, span(c)] for ref in got_refs])
            before = start_ref[c]
            after = jnp.maximum(0.0, before + step_size * (scale * total))
            x_one_ref[:, span(c)] = after
            moved += (after - before) ** 2
            put_block(right_ref, c, scale * (2.0 * after - before))
        moved_ref[...] = moved

        for ref in (out_ref, out_two_ref):
            ref[...] = jnp.zeros_like(ref)
        tile_pass(meta_ref, count_ref, turned_ref, right_ref, False, (out_ref, out_two_ref))

        moved = jnp.zeros((VECS, EDGE), jnp.float32)
        for r in range(ROWBLK):
            scale = rscale_ref[r : r + 1, :]
            before = both_ref[:, span(r)]
            after = jnp.maximum(
                0.0, before + step_size * (scale * (bound_ref[:, span(r)] - joined(out_ref[r] + out_two_ref[r])))
            )
            y_one_ref[:, span(r)] = after
            moved += (after - before) ** 2
            put_block(left_ref, r, after * scale)

        tile_pass(meta_ref, count_ref, tiles_ref, left_ref, True, sums_refs)
        for c in range(blocks):
            send_ref[:, span(c)] = adjoint_sum(sums_refs, c)
        send_ref[:, blocks * EDGE :] = moved


def last_kernel(parts, meta_ref, count_ref, turned_ref, *rest):
    got_refs = rest[:parts]
    (
        rscale_ref, y_ref, bound_ref, x_one_ref, cscale_ref, moved_ref,
        mine_ref, other_ref,
        own_ref, right_ref, out_ref, out_two_ref,
    ) = rest[parts:]
    blocks = own_ref.shape[0]
    places = blocks // VECS
    half = VECS // 2
    ncol = COLBLK * EDGE

    @pl.when(leads())
    def _():
        band = lax.axis_index("band")
        dual = functools.reduce(jnp.add, [ref[:, blocks * EDGE :] for ref in got_refs])
        dual = jnp.sum(dual, axis=1, keepdims=True)
        primal = jnp.sum(moved_ref[...], axis=1, keepdims=True)
        ratio = jnp.sqrt((dual + 1e-06) / (primal + 1e-06))
        size = step_size * jnp.sqrt((primal + 1e-06) / (dual + 1e-06))
        for c in range(blocks):
            scale = cscale_ref[c // places : c // places + 1, span(c % places)]
            total = functools.reduce(jnp.add, [ref[:, span(c)] for ref in got_refs])
            before = x_one_ref[:, span(c)]
            after = jnp.maximum(0.0, before + size * (scale * total))
            own_ref[c] = after
            put_block(right_ref, c, scale * (2.0 * after - before))
        for j in range(COLBLK):
            own = own_ref[band * COLBLK + j]
            mine_ref[:, span(j)] = own[0:half]
            other_ref[:, span(j)] = own[half:]

        for ref in (out_ref, out_two_ref):
            ref[...] = jnp.zeros_like(ref)
        tile_pass(meta_ref, count_ref, turned_ref, right_ref, False, (out_ref, out_two_ref))

        for r in range(ROWBLK):
            scale = rscale_ref[r : r + 1, :]
            after = jnp.maximum(
                0.0,
                y_ref[:, span(r)]
                + step_size * ratio * (scale * (bound_ref[:, span(r)] - joined(out_ref[r] + out_two_ref[r]))),
            )
            place = slice(ncol + r * EDGE, ncol + (r + 1) * EDGE)
            mine_ref[:, place] = after[0:half]
            other_ref[:, place] = after[half:]


def finish_kernel(mine_ref, got_ref, x_ref, y_ref, sems):
    ncol = x_ref.shape[1]

    def give(from_ref):
        copies = [
            pltpu.make_async_copy(from_ref.at[:, 0:ncol], x_ref, sems.at[0]),
            pltpu.make_async_copy(from_ref.at[:, ncol:], y_ref, sems.at[1]),
        ]
        for copy in copies:
            copy.start()
        for copy in copies:
            copy.wait()

    pl.when(leads())(lambda: give(mine_ref))
    pl.when(jnp.logical_not(leads()))(lambda: give(got_ref))


def swap(value):
    count = lax.axis_size("batch")
    return lax.ppermute(value, "batch", [(i, i ^ 1) for i in range(count)])


def relayed(value, hop, side):
    bands, batches = lax.axis_size("band"), lax.axis_size("batch")
    pairs = []
    for band in range(bands):
        for batch in range(batches):
            to = band ^ hop if batch % 2 == side else band
            pairs.append((band * batches + batch, to * batches + (batch ^ 1)))
    return lax.ppermute(value, ("band", "batch"), pairs)


def gathered(value, hops, side):
    return [swap(value)] + [relayed(value, hop, side) for hop in hops]


def rounds_of(bands):
    rounds, bit = [], 1
    while bit < bands:
        if bit * 2 < bands:
            rounds.append((bit, 2 * bit, 3 * bit))
        else:
            rounds.append((bit,))
        bit *= 4
    return rounds if len(rounds) % 2 == 0 else rounds + [()]


def shards(tiles, tile_row, tile_col, tile_count, cost, bound_vec, x_start, y_start):
    tiles = tiles[0]
    ntile = tiles.shape[0]
    bands = lax.axis_size("band")
    blocks = bands * COLBLK
    head = (blocks + blocks // VECS) * EDGE
    bound = bound_vec.reshape(1, -1)
    nrow = bound.shape[1]
    f32 = lambda *shape: jax.ShapeDtypeStruct(shape, jnp.float32)
    v32 = lambda *shape: pltpu.VMEM(shape, jnp.float32)
    v16 = lambda *shape: pltpu.VMEM(shape, jnp.bfloat16)
    smem = [pl.BlockSpec(memory_space=pltpu.SMEM)]
    hbm = lambda n: [pl.BlockSpec(memory_space=pltpu.HBM)] * n
    vmem = lambda n: [pl.BlockSpec(memory_space=pltpu.VMEM)] * n
    left = [v16(2 * (ROWBLK + 1), 2 * KEPT, EDGE)]
    right = [v32(blocks, VECS, EDGE), v16(2 * blocks, 2 * KEPT, EDGE)]
    rows_out = [v32(ROWBLK + 1, KEPT, EDGE)] * 2
    sums = [v32(blocks, KEPT, EDGE)] * 2
    params = pltpu.CompilerParams(vmem_limit_bytes=32 * 1024 * 1024)
    in_hbm = lambda value: pltpu.with_memory_space_constraint(value, pltpu.HBM)

    tile_cost = pl.CostEstimate(flops=0, bytes_accessed=tiles.nbytes, transcendentals=0)
    meta, mine, held, spread, rscale = pl.pallas_call(
        scale_kernel,
        out_shape=(
            pltpu.SMEM((2, ntile), jnp.int32),
            v32(VECS // 2, nrow + 2 * COLBLK * EDGE),
            v16(*tiles.shape),
            v32(ROWBLK + 1, EDGE, EDGE),
            v32(ROWBLK, EDGE),
        ),
        in_specs=hbm(2) + smem + hbm(4),
        out_specs=tuple(smem + vmem(4)),
        scratch_shapes=[
            pltpu.SemaphoreType.DMA((5,)),
            pltpu.SemaphoreType.DMA((ntile // FETCH,)),
            v16(ROWBLK + 1, EDGE, EDGE),
            v16(ROWBLK + 1, EDGE, EDGE),
        ],
        compiler_params=params,
        cost_estimate=tile_cost,
        name="row_scales",
    )(in_hbm(tile_row), in_hbm(tile_col), tile_count, *map(in_hbm, (y_start, x_start, cost, tiles)))
    other = swap(mine)

    top = pl.pallas_call(
        columns_kernel,
        out_shape=v32(blocks, EDGE),
        in_specs=smem * 2 + vmem(2),
        out_specs=vmem(1)[0],
        scratch_shapes=[v32(blocks, 8, EDGE)] * 2,
        compiler_params=params,
        cost_estimate=tile_cost,
        name="columns",
    )(meta, tile_count, held, spread)

    turned = pl.pallas_call(
        turn_kernel,
        out_shape=v16(*tiles.shape),
        in_specs=vmem(1),
        out_specs=vmem(1)[0],
        compiler_params=params,
        cost_estimate=tile_cost,
        name="turn",
    )(held)

    message, both = pl.pallas_call(
        start_kernel,
        out_shape=(f32(VECS, head + COLBLK * EDGE), v32(VECS, mine.shape[1])),
        in_specs=smem * 2 + vmem(5),
        out_specs=tuple(vmem(2)),
        scratch_shapes=left + sums,
        compiler_params=params,
        name="start",
    )(meta, tile_count, held, rscale, top, mine, other)

    rounds = rounds_of(bands)
    offsets = [0]
    for index, hops in enumerate(rounds):
        messages = gathered(message, hops, (index + 1) % 2)
        offsets = [hop ^ offset for hop in (0, *hops) for offset in offsets]
        if index < len(rounds) - 1:
            message = pl.pallas_call(
                functools.partial(merge_kernel, blocks),
                out_shape=f32(VECS, head + len(offsets) * COLBLK * EDGE),
                in_specs=vmem(len(messages)),
                out_specs=vmem(1)[0],
                compiler_params=params,
                name="merge",
            )(*messages)

    message, x_one, cscale, y_one, moved = pl.pallas_call(
        functools.partial(step_kernel, offsets, len(messages)),
        out_shape=(
            f32(VECS, (blocks + 1) * EDGE), v32(VECS, blocks * EDGE), v32(VECS, blocks // VECS * EDGE), v32(VECS, nrow), v32(VECS, EDGE),
        ),
        in_specs=smem * 2 + vmem(5 + len(messages)),
        out_specs=tuple(vmem(5)),
        scratch_shapes=right + rows_out + left + sums,
        compiler_params=params,
        name="first_step",
    )(meta, tile_count, held, turned, *messages, rscale, both, bound)

    for index, hops in enumerate(rounds):
        messages = gathered(message, hops, (index + 1) % 2)
        if index < len(rounds) - 1:
            message = functools.reduce(jnp.add, messages)

    half = VECS // 2
    width = COLBLK * EDGE + nrow
    mine, other = pl.pallas_call(
        functools.partial(last_kernel, len(messages)),
        out_shape=(v32(half, width), v32(half, width)),
        in_specs=smem * 2 + vmem(7 + len(messages)),
        out_specs=tuple(vmem(2)),
        scratch_shapes=right + rows_out,
        compiler_params=params,
        name="second_step",
    )(meta, tile_count, turned, *messages, rscale, y_one, bound, x_one, cscale, moved)

    return pl.pallas_call(
        finish_kernel,
        out_shape=(f32(*x_start.shape), f32(*y_start.shape)),
        in_specs=vmem(2),
        out_specs=tuple(hbm(2)),
        scratch_shapes=[pltpu.SemaphoreType.DMA((2,))],
        compiler_params=params,
        name="finish",
    )(mine, pltpu.with_memory_space_constraint(swap(other), pltpu.VMEM))


def solution(mesh):
    return jax.shard_map(
        shards,
        mesh=mesh,
        in_specs=(
            P("band", None, None, None),
            P("band", None),
            P("band", None),
            P("band"),
            P("batch", "band"),
            P("band"),
            P("batch", "band"),
            P("batch", "band"),
        ),
        out_specs=(P("batch", "band"), P("batch", "band")),
        check_vma=False,
    )
```
